32 devices in a mesh: ctx: 8 (over z, x), req: 4 (over y, core).
Axes of the slice: x: 2, y: 2, z: 4, core: 2. Of those that a mesh axis runs over, the one named last changes fastest.
Arguments:
- latents: bfloat16 [16, 16384, 576], P('req', 'ctx'), may hold values from -6 to 6
- index_keys: bfloat16 [16, 16384, 128], P('req', 'ctx'), may hold values from -6 to 6
- queries: bfloat16 [4, 16, 128, 576], P(None, 'req', 'ctx'), may hold values from -72 to 72
- index_queries: bfloat16 [4, 16, 64, 128], P(None, 'req', 'ctx'), may hold values from -0.5 to 0.5
- index_weights: bfloat16 [4, 16, 64], P(None, 'req', 'ctx'), may hold values from -1.5 to 1.5
- value_up_weight: bfloat16 [128, 512, 128], P('ctx', 'req'), may hold values from -0.75 to 0.75
- selection: int32 [4, 16, 32], P(None, 'req'), may hold values from 0 to 255, as said below
- counts: int32 [4, 16], P(None, 'req'), may hold values from 21 to 32, as said below
- lengths: int32 [16], P('req'), may hold values from 8192 to 16380, as said below
Outputs:
- head_values: bfloat16 [4, 16, 128, 128], P(None, 'req', 'ctx')
- index_scores: float32 [4, 16, 16384], P(None, 'req', 'ctx')
The draws below stay inside these ranges and needn't reach their ends.
Inputs may be any that keep to these rules, and one draw needn't show every extreme that they name: Context lengths; every step's query position lengths[r] + s lies in the context. `selection`: the first counts[s, r] slots name different blocks, each holding a live position of that step; every list holds the block of the step's own position and at least one block whose positions are all live; later slots hold 0. Of the blocks that one device's context shard holds, at most 8 are named in one list. `counts`: live slots of a list.
All inputs are finite; a program needn't handle non-finite values.
Results may differ from the reference program's by a relative error of at most 0.018.
Values may be sent and summed in bfloat16 or wider, within the bound.
No kernel may reach another device: no remote copies, remote signals or barrier semaphores. Data moves between devices by JAX's collectives and lax.ppermute only.
A program may use at most 128 MiB of HBM per device.

```python
import jax
import jax.numpy as jnp
from jax import lax

HEADS = 128
KV = 512
ROPE = 64
VDIM = 128
IHEADS = 64
IDX_DIM = 128
QK_DIM = 192
BLOCK = 64
SEL = 32
STEPS = 4
CTX_DEV = 2048
MOST = 8
REQS = 16
CTX = 16384


def selection_plan(key):
    key = jax.random.fold_in(key, 11)
    subkeys = jax.random.split(key, 8)
    blocks_dev = CTX_DEV // BLOCK
    lengths = jax.random.randint(subkeys[0], (REQS,), CTX // 2, CTX - STEPS + 1)
    longest = jax.random.randint(subkeys[1], (), 0, REQS)
    lengths = lengths.at[longest].set(CTX - STEPS)
    lengths = lengths.at[(longest + 1) % REQS].set(CTX // 2)
    step_ids = jnp.arange(STEPS, dtype=jnp.int32)
    current_step = (lengths[None, :] + step_ids[:, None]) // BLOCK
    whole_shards = current_step // blocks_dev
    hot_shard = jax.random.randint(subkeys[2], (STEPS, REQS), 0, 1 << 20) % whole_shards
    hot_start = jax.random.randint(subkeys[3], (STEPS, REQS), 0, blocks_dev)
    hot_rank = jnp.arange(MOST, dtype=jnp.int32)
    hot_blocks = hot_shard[..., None] * blocks_dev + (hot_start[..., None] + hot_rank) % blocks_dev
    other_count = SEL - MOST - 1
    turn_offset = jax.random.randint(subkeys[4], (STEPS, REQS), 0, 1 << 20)
    other_rank = jnp.arange(other_count, dtype=jnp.int32) + turn_offset[..., None]
    shards_left = whole_shards[..., None] - 1
    other_shard = (hot_shard[..., None] + 1 + other_rank % shards_left) % whole_shards[..., None]
    other_start = jax.random.randint(subkeys[5], (STEPS, REQS), 0, blocks_dev)
    other_blocks = other_shard * blocks_dev + (other_start[..., None] + other_rank // shards_left) % blocks_dev
    listed = jnp.concatenate([hot_blocks, current_step[..., None], other_blocks], axis=-1)
    shortfall = jax.random.randint(subkeys[6], (STEPS, REQS), 0, other_count // 2 + 1)
    shortfall = shortfall.at[0, 0].set(0)
    shortfall = shortfall.at[STEPS - 1, REQS - 1].set(other_count // 2)
    counts = SEL - shortfall
    slot_ids = jnp.arange(SEL, dtype=jnp.int32)
    listed = jnp.where(slot_ids < counts[..., None], listed, 0)
    order_key = jax.random.randint(subkeys[7], (STEPS, REQS, SEL), 0, 1 << 16) * SEL + slot_ids
    order_key = jnp.where(slot_ids < counts[..., None], order_key, (1 << 22) + slot_ids)
    order = jnp.argsort(order_key, axis=-1, stable=True)
    selection = jnp.take_along_axis(listed, order, axis=-1)
    return (lengths, selection, counts)


def draw_lengths(key, part):
    lengths, selection, counts = selection_plan(key)
    return lengths


def draw_selection(key, part):
    lengths, selection, counts = selection_plan(key)
    return selection


def draw_counts(key, part):
    lengths, selection, counts = selection_plan(key)
    return counts


def draw_latents(key, part):
    key = jax.random.fold_in(key, 3)
    sample = jax.random.normal(key, (REQS, CTX, KV + ROPE), jnp.float32)
    sample = jnp.clip(sample, -6.0, 6.0)
    return sample.astype(jnp.bfloat16)


def draw_queries(key, part):
    key = jax.random.fold_in(key, 5)
    sample = 1.3 * jax.random.normal(key, (STEPS, REQS, HEADS, KV + ROPE), jnp.float32)
    sample = jnp.clip(sample, -7.0, 7.0)
    return sample.astype(jnp.bfloat16)


def steps_of(rng, shape, pieces, low, top_value):
    level = 1.0
    for axis_at, parts in pieces:
        heights = jax.random.uniform(jax.random.fold_in(jax.random.fold_in(rng, 6), axis_at), (parts,), jnp.float32, low / len(pieces), top_value / len(pieces))
        level = level * jnp.repeat(jnp.exp(heights), shape[axis_at] // parts).reshape((-1,) + (1,) * (len(shape) - 1 - axis_at))
    return level


def centred(stream_key, dims, scale, most, cuts=(), held_as=jnp.bfloat16):
    drawn = scale * jax.random.normal(stream_key, dims, jnp.float32)
    if cuts:
        drawn = drawn * steps_of(stream_key, dims, cuts, -0.22, 0.18)
    return jnp.clip(drawn, -most, most).astype(held_as)


def setup_inputs(seed: int = 0) -> dict:
    arg_keys = jax.random.split(jax.random.key(seed), 10)
    return {
        "latents": draw_latents(jax.random.fold_in(arg_keys[9], 71), 0),
        "index_keys": centred(arg_keys[1], (REQS, CTX, IDX_DIM), 1.0, 6.0, ((0, 4), (1, 8))),
        "queries": draw_queries(jax.random.fold_in(arg_keys[9], 71), 0),
        "index_queries": centred(arg_keys[3], (STEPS, REQS, IHEADS, IDX_DIM), IDX_DIM ** -0.5, 0.5, ((1, 4), (2, 8))),
        "index_weights": centred(arg_keys[4], (STEPS, REQS, IHEADS), 0.25, 1.5, ((1, 4), (2, 8))),
        "value_up_weight": centred(arg_keys[5], (HEADS, KV, VDIM), (KV // 8) ** -0.5, 0.75, ((0, 8), (1, 4))),
        "selection": draw_selection(jax.random.fold_in(arg_keys[9], 71), 0),
        "counts": draw_counts(jax.random.fold_in(arg_keys[9], 71), 0),
        "lengths": draw_lengths(jax.random.fold_in(arg_keys[9], 71), 0),
    }


def reference(latents, index_keys, queries, index_queries, index_weights, value_up_weight, selection, counts, lengths):
    score_scale = QK_DIM ** -0.5
    step_ids = jnp.arange(STEPS, dtype=jnp.int32)

    def index_request(request):
        queries_here = index_queries[:, request].reshape(STEPS * IHEADS, IDX_DIM)
        products = jnp.dot(queries_here, index_keys[request].T, preferred_element_type=jnp.float32)
        products = jnp.maximum(products, 0.0).reshape(STEPS, IHEADS, CTX)
        weighting = index_weights[:, request].astype(jnp.float32)
        summed = jnp.einsum('shc,sh->sc', products, weighting)
        positions = jnp.arange(CTX, dtype=jnp.int32)
        limits = lengths[request] + step_ids
        return jnp.where(positions[None, :] <= limits[:, None], summed, 0.0)

    index_scores = lax.map(index_request, jnp.arange(REQS, dtype=jnp.int32))
    index_scores = jnp.transpose(index_scores, (1, 0, 2))

    def attend_pair(pair):
        step_id = pair[0]
        request = pair[1]
        chosen = selection[step_id, request]
        block_tiles = latents[request].reshape(CTX // BLOCK, BLOCK, KV + ROPE)
        gathered = jnp.take(block_tiles, chosen, axis=0).reshape(SEL * BLOCK, KV + ROPE)
        positions = (chosen[:, None] * BLOCK + jnp.arange(BLOCK, dtype=jnp.int32)[None, :]).reshape(SEL * BLOCK)
        in_list = jnp.repeat(jnp.arange(SEL, dtype=jnp.int32) < counts[step_id, request], BLOCK)
        usable = in_list & (positions <= lengths[request] + step_id)
        scores = jnp.dot(queries[step_id, request], gathered.T, preferred_element_type=jnp.float32) * score_scale
        scores = jnp.where(usable[None, :], scores, -1e30)
        peak_score = jnp.max(scores, axis=1, keepdims=True)
        exp_weights = jnp.where(usable[None, :], jnp.exp(scores - peak_score), 0.0)
        row_total = jnp.sum(exp_weights, axis=1, keepdims=True)
        mixed_rows = jnp.dot(exp_weights.astype(jnp.bfloat16), gathered[:, :KV], preferred_element_type=jnp.float32)
        return (mixed_rows / row_total).astype(jnp.bfloat16)

    step_grid = jnp.repeat(step_ids, REQS)
    request_grid = jnp.tile(jnp.arange(REQS, dtype=jnp.int32), STEPS)
    attended_output = lax.map(attend_pair, jnp.stack([step_grid, request_grid], axis=1))
    lifted_values = jnp.einsum('drg,rgu->dru', attended_output.astype(jnp.float32), value_up_weight.astype(jnp.float32))
    head_values = lifted_values.astype(jnp.bfloat16).reshape(STEPS, REQS, HEADS, VDIM)
    return head_values, index_scores
```

```python
import functools

import jax
import jax.numpy as jnp
from jax import lax
from jax.experimental import pallas as pl
from jax.experimental.pallas import tpu as pltpu
from jax.sharding import PartitionSpec as P

KV = 512
QK_DIM = 192
BLOCK = 64
VMEM_LIMIT = 40 * 1024 * 1024

CHUNKS = 2
PAIRS = 8
HEADS = 16
ROWS = PAIRS * HEADS
EXTRA = 8
WIDE = 640
SLOTS = 8
LANES = 128


def compact_slots(owned_slot, local_block, capacity):
    ranking = jnp.cumsum(owned_slot.astype(jnp.int32), axis=-1) - 1
    places = jnp.arange(capacity, dtype=jnp.int32)
    chosen = (owned_slot[..., None, :] & (ranking[..., None, :] == places[:, None])).astype(
        jnp.int32
    )
    block_index = jnp.sum(chosen * local_block[..., None, :], axis=-1)
    filled = jnp.sum(chosen, axis=-1) > 0
    return (block_index, filled)


def call(body, **kwargs):
    return pl.pallas_call(
        body,
        compiler_params=pltpu.CompilerParams(vmem_limit_bytes=VMEM_LIMIT),
        **kwargs,
    )


def whole(shape):
    return pl.BlockSpec(shape, lambda *_: (0,) * len(shape))


def pack_kernel(q_ref, iq_ref, iw_ref, out_ref):
    for step in range(4):
        for local in range(2):
            row = (step * 2 + local) * HEADS
            query = q_ref[step, local]
            index_query = iq_ref[step, local]
            halves = jnp.concatenate([index_query[:, :64], index_query[:, 64:]], axis=0)
            out_ref[row : row + HEADS, :512] = query[:, :512]
            out_ref[row : row + HEADS, 512:] = jnp.concatenate([query[:, 512:], halves], axis=1)
    out_ref[ROWS:, :] = jnp.zeros((EXTRA, WIDE), jnp.bfloat16)
    out_ref[ROWS:, :LANES] = iw_ref[...]


def pack(chunk, queries, index_queries, weight_columns):
    return call(
        pack_kernel,
        grid=(1,),
        in_specs=[
            pl.BlockSpec((4, 2, HEADS, 576), lambda _: (0, chunk, 0, 0)),
            pl.BlockSpec((4, 2, 8, 128), lambda _: (0, chunk, 0, 0)),
            whole((8, LANES)),
        ],
        out_specs=whole((ROWS + EXTRA, WIDE)),
        out_shape=jax.ShapeDtypeStruct((ROWS + EXTRA, WIDE), jnp.bfloat16),
        name="pack",
    )(queries, index_queries, weight_columns)


def gather_kernel(chunk, block_ref, latent_ref, out_ref):
    request = chunk * 2 + pl.program_id(0)
    first_half = lax.broadcasted_iota(jnp.int32, (576, LANES), 1) < 64

    def tile(step, slot, want_odd):
        block = block_ref[step, request, slot]
        start = pl.multiple_of((block // 2) * LANES, LANES)
        here = latent_ref[0, :, pl.ds(start, LANES)]
        turned = jnp.concatenate([here[:, 64:], here[:, :64]], axis=1)
        return jnp.where(block % 2 == want_odd, here, turned)

    for step in range(4):
        for half in range(SLOTS // 2):
            left = tile(step, 2 * half, 0)
            right = tile(step, 2 * half + 1, 1)
            out_ref[step, 0, :576, half * LANES : (half + 1) * LANES] = jnp.where(
                first_half, left, right
            )
        out_ref[step, 0, 576:, :] = jnp.zeros((64, 512), jnp.bfloat16)


def gather(chunk, block_index, latents_t):
    return call(
        functools.partial(gather_kernel, chunk),
        grid_spec=pltpu.PrefetchScalarGridSpec(
            num_scalar_prefetch=1,
            grid=(2,),
            in_specs=[pl.BlockSpec((1, 576, 2048), lambda i, _: (chunk * 2 + i, 0, 0))],
            out_specs=pl.BlockSpec((4, 1, WIDE, 512), lambda i, _: (0, i, 0, 0)),
        ),
        out_shape=jax.ShapeDtypeStruct((4, 2, WIDE, 512), jnp.bfloat16),
        name="gather_blocks",
    )(block_index, latents_t)


def split3(value):
    high = value.astype(jnp.bfloat16)
    rest = value - high.astype(jnp.float32)
    middle = rest.astype(jnp.bfloat16)
    low = (rest - middle.astype(jnp.float32)).astype(jnp.bfloat16)
    return high, middle, low


def store_stats(out_ref, row, stats):
    turned = stats.T[:PAIRS]
    for place, part in enumerate(split3(turned)):
        out_ref[row : row + PAIRS, place * LANES : (place + 1) * LANES] = part
    out_ref[row : row + PAIRS, 3 * LANES :] = jnp.zeros((PAIRS, LANES), jnp.bfloat16)


def load_stats(in_ref, row):
    parts = [
        in_ref[row : row + PAIRS, place * LANES : (place + 1) * LANES].astype(jnp.float32)
        for place in range(3)
    ]
    turned = (parts[0] + parts[1]) + parts[2]
    return jnp.concatenate([turned, jnp.zeros((LANES - PAIRS, LANES), jnp.float32)], axis=0).T


def attend_kernel(*refs):
    q_refs = refs[:8]
    block_ref, bias_ref = refs[8:10]
    own_a, own_b, send_a, send_b, stats_ref = refs[10:]
    step = pl.program_id(0)
    lane = lax.broadcasted_iota(jnp.int32, (LANES, LANES), 1)

    @pl.when(step == 0)
    def _():
        stats_ref[...] = jnp.zeros((LANES, LANES), jnp.float32)

    stats = stats_ref[...]
    for local in range(2):
        query = jnp.concatenate([r[local * HEADS : (local + 1) * HEADS, :] for r in q_refs], axis=0)
        blocks = block_ref[0, local]
        scores = jnp.dot(query, blocks, preferred_element_type=jnp.float32) * (QK_DIM**-0.5)
        scores = scores + bias_ref[0, local]
        peak = jnp.maximum(jnp.max(scores, axis=1, keepdims=True), -1e29)
        weights = jnp.exp(scores - peak)
        total = jnp.maximum(jnp.sum(weights, axis=1, keepdims=True), 1e-30)
        mixed = lax.dot_general(
            weights.astype(jnp.bfloat16),
            blocks[:KV],
            (((1,), (1,)), ((), ())),
            preferred_element_type=jnp.float32,
        )
        mixed = (mixed * (1.0 / total)).astype(jnp.bfloat16)
        pair = step * 2 + local
        stats = jnp.where(lane == pair, peak + jnp.log(total), stats)
        for across, (out_a, out_b) in enumerate(((own_a, own_b), (send_a, send_b))):
            for out, members in ((out_a, (3, 2)), (out_b, (1, 0))):
                for place, member in enumerate(members):
                    source = (across * 4 + member) * HEADS
                    row = pl.multiple_of(place * ROWS + pair * HEADS, HEADS)
                    out[pl.ds(row, HEADS), :] = mixed[source : source + HEADS]
    stats_ref[...] = stats

    @pl.when(step == 3)
    def _():
        store_stats(send_a, 2 * ROWS, stats)


def attend(gathered_queries, blocks, bias):
    bf16 = jnp.bfloat16
    return call(
        attend_kernel,
        grid=(4,),
        in_specs=[pl.BlockSpec((2 * HEADS, WIDE), lambda i: (i, 0))] * 8
        + [
            pl.BlockSpec((1, 2, WIDE, 512), lambda i: (i, 0, 0, 0)),
            pl.BlockSpec((1, 2, 1, 512), lambda i: (i, 0, 0, 0)),
        ],
        out_specs=[
            whole((2 * ROWS, KV)),
            whole((2 * ROWS, KV)),
            whole((2 * ROWS + EXTRA, KV)),
            whole((2 * ROWS, KV)),
            whole((LANES, LANES)),
        ],
        out_shape=[
            jax.ShapeDtypeStruct((2 * ROWS, KV), bf16),
            jax.ShapeDtypeStruct((2 * ROWS, KV), bf16),
            jax.ShapeDtypeStruct((2 * ROWS + EXTRA, KV), bf16),
            jax.ShapeDtypeStruct((2 * ROWS, KV), bf16),
            jax.ShapeDtypeStruct((LANES, LANES), jnp.float32),
        ],
        name="attend",
    )(*gathered_queries, blocks, bias)


def joined(own_ref, other_ref, place, weight_own, weight_other):
    for pair in range(PAIRS):
        row = place * ROWS + pair * HEADS
        own = own_ref[row : row + HEADS, :].astype(jnp.float32)
        other = other_ref[row : row + HEADS, :].astype(jnp.float32)
        yield pair, (
            own * weight_own[:, pair : pair + 1] + other * weight_other[:, pair : pair + 1]
        )


def join_a_kernel(own_ref, other_ref, stats_ref, out3_ref, out2_ref, weight_ref, lse_ref):
    own = stats_ref[:64]
    other = load_stats(other_ref, 2 * ROWS)[64:]
    peak = jnp.maximum(own, other)
    own, other = jnp.exp(own - peak), jnp.exp(other - peak)
    total = own + other
    own, other = own / total, other / total
    lse = jnp.concatenate([peak + jnp.log(total), jnp.zeros((64, LANES), jnp.float32)], axis=0)
    weight_ref[0] = own
    weight_ref[1] = other
    lse_ref[...] = lse
    for place, (member, out_ref) in enumerate(((3, out3_ref), (2, out2_ref))):
        part = slice(member * HEADS, (member + 1) * HEADS)
        for pair, rows in joined(own_ref, other_ref, place, own[part], other[part]):
            out_ref[pair * HEADS : (pair + 1) * HEADS, :] = rows.astype(jnp.bfloat16)
        store_stats(out_ref, ROWS, lse)


def join_a(own, other, stats):
    message = jax.ShapeDtypeStruct((ROWS + EXTRA, KV), jnp.bfloat16)
    return call(
        join_a_kernel,
        out_shape=[
            message,
            message,
            jax.ShapeDtypeStruct((2, 64, LANES), jnp.float32),
            jax.ShapeDtypeStruct((LANES, LANES), jnp.float32),
        ],
        name="join_far",
    )(own, other, stats)


def join_b_kernel(own_ref, other_ref, weight_ref, lse_ref, out1_ref, out0_ref):
    for place, (member, out_ref) in enumerate(((1, out1_ref), (0, out0_ref))):
        part = slice(member * HEADS, (member + 1) * HEADS)
        weights = weight_ref[0, part], weight_ref[1, part]
        for pair, rows in joined(own_ref, other_ref, place, *weights):
            out_ref[pair * HEADS : (pair + 1) * HEADS, :] = rows.astype(out_ref.dtype)
    store_stats(out1_ref, ROWS, lse_ref[...])


def join_b(own, other, weights, lse):
    return call(
        join_b_kernel,
        out_shape=[
            jax.ShapeDtypeStruct((ROWS + EXTRA, KV), jnp.bfloat16),
            jax.ShapeDtypeStruct((ROWS, KV), jnp.float32),
        ],
        name="join_near",
    )(own, other, weights, lse)


def finish_kernel(lse_ref, own_ref, r1_ref, r2_ref, r3_ref, up_ref, *rest):
    out_ref, rows_ref, lifted_ref = rest[-3:]
    received = (r1_ref, r2_ref, r3_ref)
    stats = [lse_ref[:HEADS]] + [
        load_stats(ref, ROWS)[member * HEADS : (member + 1) * HEADS]
        for member, ref in enumerate(received, 1)
    ]
    peak = functools.reduce(jnp.maximum, stats)
    stats = [jnp.exp(value - peak) for value in stats]
    total = functools.reduce(jnp.add, stats)
    stats = [value / total for value in stats]
    for pair in range(PAIRS):
        part = slice(pair * HEADS, (pair + 1) * HEADS)
        rows = own_ref[part, :] * stats[0][:, pair : pair + 1]
        for value, ref in zip(stats[1:], received):
            rows = rows + ref[part, :].astype(jnp.float32) * value[:, pair : pair + 1]
        for tile in range(4):
            rows_ref[tile, part, :] = rows[:, tile * LANES : (tile + 1) * LANES]
    for head in range(HEADS):
        attended = jnp.concatenate(
            [rows_ref[tile, pl.ds(head, PAIRS, stride=HEADS), :] for tile in range(4)], axis=1
        ).astype(jnp.bfloat16)
        lifted_ref[pl.ds(head, PAIRS, stride=HEADS), :] = jnp.dot(
            attended, up_ref[head], preferred_element_type=jnp.float32
        )
    for step in range(4):
        for local in range(2):
            row = (step * 2 + local) * HEADS
            out_ref[step, local] = lifted_ref[row : row + HEADS, :].astype(jnp.bfloat16)


def finish(chunk, lse, own, received, up, before):
    message = whole((ROWS + EXTRA, KV))
    specs = [whole((LANES, LANES)), whole((ROWS, KV)), message, message, message]
    specs.append(whole((HEADS, KV, 128)))
    args = [lse, own, *received, up]
    aliases = {}
    if before is not None:
        specs.append(pl.BlockSpec(memory_space=pl.ANY))
        args.append(before)
        aliases = {len(args) - 1: 0}
    return call(
        finish_kernel,
        grid=(1,),
        in_specs=specs,
        out_specs=pl.BlockSpec((4, 2, HEADS, 128), lambda _: (0, chunk, 0, 0)),
        out_shape=jax.ShapeDtypeStruct((4, 4, HEADS, 128), jnp.bfloat16),
        scratch_shapes=[
            pltpu.VMEM((4, ROWS, LANES), jnp.float32),
            pltpu.VMEM((ROWS, 128), jnp.float32),
        ],
        input_output_aliases=aliases,
        name="finish",
    )(*args)


def assemble_kernel(place_ref, *refs):
    out_ref = refs[-1]
    for relative, ref in enumerate(refs[:-1]):
        start = pl.multiple_of((place_ref[0] ^ relative) * 128, 128)
        out_ref[:, pl.ds(start, 128), :] = ref[...]


def assemble(place, pieces):
    return call(
        assemble_kernel,
        in_specs=[pl.BlockSpec(memory_space=pltpu.SMEM)] + [pl.BlockSpec()] * 4,
        out_shape=jax.ShapeDtypeStruct((HEADS, KV, 128), jnp.bfloat16),
        name="assemble_up",
    )(place, *pieces)


def index_kernel(scalar_ref, *refs):
    payloads = refs[:8], refs[8:16]
    key_ref, out_ref = refs[16:]
    request = pl.program_id(0)
    local = request % 2
    base = scalar_ref[4]
    limit = scalar_ref[request]
    for chunk in range(CHUNKS):

        @pl.when(request // 2 == chunk)
        def _(members=payloads[chunk]):
            columns = jnp.concatenate([r[ROWS:, :LANES] for r in members], axis=0)
            columns = columns.astype(jnp.float32)
            lane = lax.broadcasted_iota(jnp.int32, (64, LANES), 1)
            query_rows, weight_rows = [], []
            for step in range(4):
                pair = step * 2 + local
                row = pl.multiple_of(pair * HEADS, HEADS)
                tail = jnp.concatenate(
                    [r[pl.ds(row, HEADS), 512:] for r in members], axis=0
                ).astype(jnp.float32)
                tail = tail.reshape(8, 2, 8, LANES)
                first = tail[:, 0].reshape(64, LANES)
                second = tail[:, 1].reshape(64, LANES)
                query_rows.append(jnp.concatenate([first[:, 64:], second[:, 64:]], axis=1))
                weight_rows.append(
                    jnp.sum(jnp.where(lane == pair, columns, 0.0), axis=1, keepdims=True)
                )
            queries = jnp.concatenate(query_rows, axis=0).astype(jnp.bfloat16)
            for part in range(4):
                at = slice(part * 512, (part + 1) * 512)
                products = lax.dot_general(
                    queries,
                    key_ref[0, at, :],
                    (((1,), (1,)), ((), ())),
                    preferred_element_type=jnp.float32,
                )
                position = base + part * 512 + lax.broadcasted_iota(jnp.int32, (1, 512), 1)
                for step in range(4):
                    mine = jnp.maximum(products[step * 64 : (step + 1) * 64], 0.0)
                    summed = jnp.sum(mine * weight_rows[step], axis=0, keepdims=True)
                    out_ref[step, pl.ds(request, 1), at] = jnp.where(
                        position <= limit + step, summed, 0.0
                    )


def index_rows(scalars, payloads, index_keys):
    return call(
        index_kernel,
        grid_spec=pltpu.PrefetchScalarGridSpec(
            num_scalar_prefetch=1,
            grid=(4,),
            in_specs=[whole((ROWS + EXTRA, WIDE))] * 16
            + [pl.BlockSpec((1, 2048, 128), lambda i, _: (i, 0, 0))],
            out_specs=whole((4, 4, 2048)),
        ),
        out_shape=jax.ShapeDtypeStruct((4, 4, 2048), jnp.float32),
        name="index_scores",
    )(scalars, *payloads[0], *payloads[1], index_keys)


def fast(
    latents,
    index_keys,
    queries,
    index_queries,
    index_weights,
    value_up_weight,
    selection,
    counts,
    lengths,
):
    own_shard = lax.axis_index("ctx")
    context_dev = latents.shape[1]
    blocks_dev = context_dev // BLOCK

    def across_x(value):
        return lax.ppermute(value, "ctx", [(i, i ^ 1) for i in range(8)])

    def across_z(value, distance):
        return lax.ppermute(value, "ctx", [(i, i ^ (2 * distance)) for i in range(8)])

    def across_req(value, distance):
        return lax.ppermute(value, "req", [(i, i ^ distance) for i in range(4)])

    columns = index_weights.reshape(4, 2, 2, 8).transpose(1, 3, 0, 2).reshape(CHUNKS, 8, PAIRS)
    columns = jnp.pad(columns, ((0, 0), (0, 0), (0, LANES - PAIRS)))

    gathered = []
    for chunk in range(CHUNKS):
        own = pack(chunk, queries, index_queries, columns[chunk])
        z2 = across_z(own, 2)
        z1 = across_z(own, 1)
        z3 = across_z(z2, 1)
        line = [own, z1, z2, z3]
        gathered.append(line + [across_x(member) for member in line])

    local_block = selection - own_shard * blocks_dev
    slot_ids = jnp.arange(selection.shape[2], dtype=jnp.int32)
    owned_slot = (
        (local_block >= 0)
        & (local_block < blocks_dev)
        & (slot_ids[None, None, :] < counts[:, :, None])
    )
    block_index, filled = compact_slots(owned_slot, local_block, SLOTS)
    limits = lengths[None, :] + jnp.arange(4, dtype=jnp.int32)[:, None]
    positions = (block_index + own_shard * blocks_dev)[..., None] * BLOCK + jnp.arange(
        BLOCK, dtype=jnp.int32
    )
    usable = filled[..., None] & (positions <= limits[:, :, None, None])
    bias = jnp.where(usable, 0.0, -1e30).astype(jnp.float32).reshape(4, 4, 1, SLOTS * BLOCK)

    latents_t = jnp.transpose(latents, (0, 2, 1))
    up_core = across_req(value_up_weight, 1)
    up_y = across_req(value_up_weight, 2)
    up_both = across_req(up_y, 1)
    place = lax.axis_index("req").astype(jnp.int32).reshape(1)
    up = assemble(place, [value_up_weight, up_core, up_y, up_both])

    head_values = None
    for chunk in range(CHUNKS):
        blocks = gather(chunk, block_index, latents_t)
        own_a, own_b, send_a, send_b, stats = attend(
            gathered[chunk], blocks, bias[:, 2 * chunk : 2 * chunk + 2]
        )
        far3, far2, weights, lse = join_a(own_a, across_x(send_a), stats)
        near, mine = join_b(own_b, across_x(send_b), weights, lse)
        received = [across_z(near, 1), across_z(far2, 2), across_z(far3, 3)]
        head_values = finish(chunk, lse, mine, received, up, head_values)

    scalars = jnp.concatenate([lengths, (own_shard * context_dev).astype(jnp.int32).reshape(1)])
    index_scores = index_rows(scalars, gathered, index_keys)
    return (head_values, index_scores)


def per_device(
    latents,
    index_keys,
    queries,
    index_queries,
    index_weights,
    value_up_weight,
    selection,
    counts,
    lengths,
):
    own_shard = lax.axis_index("ctx")
    step_count, request_count, slot_count = selection.shape
    half_axis = lax.axis_size("ctx") // 2
    capacity = max(2, (slot_count - 2) // half_axis + 1)
    context_dev = latents.shape[1]
    row_width = latents.shape[2]
    blocks_dev = context_dev // BLOCK
    score_scale = QK_DIM ** (-0.5)
    all_query, all_index_query, all_index_weight = (
        lax.all_gather(queries, "ctx", axis=2, tiled=True),
        lax.all_gather(index_queries, "ctx", axis=2, tiled=True),
        lax.all_gather(index_weights, "ctx", axis=2, tiled=True),
    )
    step_ids = jnp.arange(step_count, dtype=jnp.int32)
    limits = lengths[None, :] + step_ids[:, None]
    token_pos = own_shard * context_dev + jnp.arange(context_dev, dtype=jnp.int32)
    products = jnp.einsum(
        "srhd,rcd->srhc", all_index_query, index_keys, preferred_element_type=jnp.float32
    )
    weighted = jnp.einsum(
        "srhc,srh->src", jnp.maximum(products, 0.0), all_index_weight.astype(jnp.float32)
    )
    index_scores = jnp.where(token_pos[None, None, :] <= limits[:, :, None], weighted, 0.0)
    local_block = selection - own_shard * blocks_dev
    slot_ids = jnp.arange(slot_count, dtype=jnp.int32)
    owned_slot = (
        (local_block >= 0)
        & (local_block < blocks_dev)
        & (slot_ids[None, None, :] < counts[:, :, None])
    )
    block_index, filled = compact_slots(owned_slot, local_block, capacity)
    block_tiles = latents.reshape(request_count, blocks_dev, BLOCK, row_width)
    request_numbers = jnp.arange(request_count, dtype=jnp.int32)[None, :, None]
    gathered = block_tiles[request_numbers, block_index].reshape(
        step_count, request_count, capacity * BLOCK, row_width
    )
    positions = (block_index + own_shard * blocks_dev)[..., None] * BLOCK + jnp.arange(
        BLOCK, dtype=jnp.int32
    )
    usable = filled[..., None] & (positions <= limits[:, :, None, None])
    usable = usable.reshape(step_count, request_count, 1, capacity * BLOCK)
    scores = (
        jnp.einsum("srhl,srtl->srht", all_query, gathered, preferred_element_type=jnp.float32)
        * score_scale
    )
    scores = jnp.where(usable, scores, -1e30)
    peak_score = jnp.max(scores, axis=-1)
    exp_weights = jnp.where(usable, jnp.exp(scores - peak_score[..., None]), 0.0)
    row_total = jnp.sum(exp_weights, axis=-1)
    mixed_rows = jnp.einsum(
        "srht,srtk->srhk",
        exp_weights.astype(jnp.bfloat16),
        gathered[..., :KV],
        preferred_element_type=jnp.float32,
    )
    global_peak = lax.pmax(peak_score, "ctx")
    shrink = jnp.exp(peak_score - global_peak)
    share_total, mixed_share = (
        lax.psum_scatter(
            (row_total * shrink).astype(jnp.bfloat16), "ctx", scatter_dimension=2, tiled=True
        ).astype(jnp.float32),
        lax.psum_scatter(
            (mixed_rows * shrink[..., None]).astype(jnp.bfloat16),
            "ctx",
            scatter_dimension=2,
            tiled=True,
        ).astype(jnp.float32),
    )
    attended_output = (mixed_share / share_total[..., None]).astype(jnp.bfloat16)
    complete_up_matrix = lax.all_gather(value_up_weight, "req", axis=1, tiled=True)
    lifted_values = jnp.einsum(
        "xefy,fym->xefm", attended_output, complete_up_matrix, preferred_element_type=jnp.float32
    )
    head_values = lifted_values.astype(jnp.bfloat16)
    return (head_values, index_scores)


def solution(mesh):
    placed = (
        P("req", "ctx", None),
        P("req", "ctx", None),
        P(None, "req", "ctx", None),
        P(None, "req", "ctx", None),
        P(None, "req", "ctx"),
        P("ctx", "req", None),
        P(None, "req", None),
        P(None, "req"),
        P("req"),
    )
    sizes = dict(mesh.shape)
    plan = fast if (sizes["ctx"], sizes["req"]) == (8, 4) else per_device
    return jax.shard_map(
        plan,
        mesh=mesh,
        in_specs=placed,
        out_specs=(P(None, "req", "ctx", None), P(None, "req", "ctx")),
        check_vma=False,
    )
```

```python
import functools

import jax
import jax.numpy as jnp
from jax import lax
from jax.experimental import pallas as pl
from jax.experimental.pallas import tpu as pltpu
from jax.sharding import PartitionSpec as P

KV = 512
QK_DIM = 192
BLOCK = 64
VMEM_LIMIT = 16 * 1024 * 1024
PACK_LIMIT = 63_000_000
ATTEND_LIMIT = 20 * 1024 * 1024
TABLE = 32
GATHER_LIMIT = 16 * 1024 * 1024
FAR = (1, 3)
NEAR = (0, 2)

CHUNKS = 2
PAIRS = 8
HEADS = 16
ROWS = PAIRS * HEADS
EXTRA = 8
SENT = ROWS + EXTRA
WIDE = 640
SLOTS = 8
LANES = 128


def call(body, limit=VMEM_LIMIT, **kwargs):
    return pl.pallas_call(
        body,
        compiler_params=pltpu.CompilerParams(vmem_limit_bytes=limit),
        **kwargs,
    )


def after(value, *earlier):
    return lax.optimization_barrier((value, *earlier))[0]


def whole(shape):
    return pl.BlockSpec(shape, lambda *_: (0,) * len(shape))


def pack_kernel(q_hbm, iq_hbm, iw_hbm, out0_ref, out1_ref, both_ref, q_ref, iq_ref, iw_ref, sems):
    small = pltpu.make_async_copy(iw_hbm, iw_ref, sems.at[4])
    small.start()
    copies = []
    for chunk in range(CHUNKS):
        requests = pl.ds(2 * chunk, 2)
        copies.append(
            (
                pltpu.make_async_copy(
                    q_hbm.at[:, requests], q_ref.at[chunk], sems.at[2 * chunk]
                ),
                pltpu.make_async_copy(
                    iq_hbm.at[:, requests], iq_ref.at[chunk], sems.at[2 * chunk + 1]
                ),
            )
        )
        for copy in copies[-1]:
            copy.start()
    small.wait()
    for chunk, out_ref in enumerate((out0_ref, out1_ref)):
        for copy in copies[chunk]:
            copy.wait()
        rows = []
        for local in range(2):
            for step in range(4):
                row = (local * 4 + step) * HEADS
                query = q_ref[chunk, step, local]
                index_query = iq_ref[chunk, step, local]
                halves = jnp.concatenate([index_query[:, :64], index_query[:, 64:]], axis=0)
                out_ref[row : row + HEADS, :512] = query[:, :512]
                out_ref[row : row + HEADS, 512:] = jnp.concatenate(
                    [query[:, 512:], halves], axis=1
                )
                request = 2 * chunk + local
                rows.append(iw_ref[step, request : request + 1, :].astype(jnp.float32))
        weights = jnp.concatenate(rows, axis=0)
        weights = jnp.concatenate([weights, jnp.zeros((PAIRS, LANES - 8), jnp.float32)], axis=1)
        out_ref[ROWS:, :LANES] = weights.astype(jnp.bfloat16)
        out_ref[ROWS:, LANES:] = jnp.zeros((EXTRA, WIDE - LANES), jnp.bfloat16)
        both_ref[chunk * SENT : (chunk + 1) * SENT, :] = out_ref[...]


def pack(queries, index_queries, index_weights):
    bf16 = jnp.bfloat16
    return call(
        pack_kernel,
        limit=PACK_LIMIT,
        in_specs=[pl.BlockSpec(memory_space=pltpu.HBM)] * 3,
        out_shape=[jax.ShapeDtypeStruct((SENT, WIDE), bf16)] * 2
        + [jax.ShapeDtypeStruct((2 * SENT, WIDE), bf16)],
        scratch_shapes=[
            pltpu.VMEM((2, 4, 2, HEADS, 576), bf16),
            pltpu.VMEM((2, 4, 2, 8, 128), bf16),
            pltpu.VMEM((4, 4, 8), bf16),
            pltpu.SemaphoreType.DMA((5,)),
        ],
        name="pack",
    )(queries, index_queries, index_weights)


def pair_up_kernel(first_ref, second_ref, out_ref):
    out_ref[:SENT, :] = first_ref[...]
    out_ref[SENT:, :] = second_ref[...]


def pair_up(first, second):
    return call(
        pair_up_kernel,
        out_shape=jax.ShapeDtypeStruct((2 * SENT, WIDE), jnp.bfloat16),
        name="pair_up",
    )(first, second)


def plan_kernel(selection_ref, counts_ref, lengths_ref, out_ref):
    shard = lax.axis_index("ctx")
    row = lax.broadcasted_iota(jnp.int32, (16, 1), 0)
    count = jnp.zeros((16, 1), jnp.int32)
    limit = jnp.zeros((16, 1), jnp.int32)
    for step in range(4):
        for request in range(4):
            here = row == step * 4 + request
            count = jnp.where(here, counts_ref[step, request], count)
            limit = jnp.where(here, lengths_ref[request] + step - shard * 2048, limit)
    selection = jnp.concatenate([selection_ref[step] for step in range(4)], axis=0)
    local = selection - shard * (2048 // BLOCK)
    slot = lax.broadcasted_iota(jnp.int32, (16, 32), 1)
    owned = (local >= 0) & (local < 2048 // BLOCK) & (slot < count)
    before = (
        lax.broadcasted_iota(jnp.int32, (32, 32), 0) < lax.broadcasted_iota(jnp.int32, (32, 32), 1)
    ).astype(jnp.float32)
    lane = lax.broadcasted_iota(jnp.int32, (16, LANES), 1)
    table = jnp.full((16, LANES), -1, jnp.int32)
    most = jnp.zeros((16, 1), jnp.int32)
    for parity in range(2):
        mine = owned & (local % 2 == parity)
        mine_f = jnp.where(mine, 1.0, 0.0)
        rank = jnp.dot(mine_f, before, preferred_element_type=jnp.float32).astype(jnp.int32)
        for place in range(SLOTS):
            chosen = mine & (rank == place)
            found = jnp.sum(jnp.where(chosen, local // 2 + 1, 0), axis=1, keepdims=True) - 1
            table = jnp.where(lane == parity * SLOTS + place, found, table)
        most = jnp.maximum(most, jnp.sum(mine_f, axis=1, keepdims=True).astype(jnp.int32))
    table = jnp.where(lane == 16, most, table)
    table = jnp.where(lane == 17, limit, table)
    out_ref[...] = table[:, :TABLE]


def plan(selection, counts, lengths):
    smem = pl.BlockSpec(memory_space=pltpu.SMEM)
    return call(
        plan_kernel,
        in_specs=[pl.BlockSpec(), smem, smem],
        out_shape=jax.ShapeDtypeStruct((16, TABLE), jnp.int32),
        name="plan",
    )(selection, counts, lengths)


def split3(value):
    high = value.astype(jnp.bfloat16)
    rest = value - high.astype(jnp.float32)
    middle = rest.astype(jnp.bfloat16)
    low = (rest - middle.astype(jnp.float32)).astype(jnp.bfloat16)
    return high, middle, low


def store_stats(out_ref, row, stats):
    turned = stats.T[:PAIRS]
    for place, part in enumerate(split3(turned)):
        out_ref[row : row + PAIRS, place * LANES : (place + 1) * LANES] = part
    out_ref[row : row + PAIRS, 3 * LANES :] = jnp.zeros((PAIRS, LANES), jnp.bfloat16)


def load_stats(in_ref, row):
    parts = [
        in_ref[row : row + PAIRS, place * LANES : (place + 1) * LANES].astype(jnp.float32)
        for place in range(3)
    ]
    turned = (parts[0] + parts[1]) + parts[2]
    return jnp.concatenate([turned, jnp.zeros((LANES - PAIRS, LANES), jnp.float32)], axis=0).T


def gather_kernel(chunk, table_ref, latent_hbm, out_ref, latent_ref, sems):
    copies = []
    for local in range(2):
        for part in range(4):
            rows = pl.ds(part * 144, 144)
            copies.append(
                pltpu.make_async_copy(
                    latent_hbm.at[2 * chunk + local, rows],
                    latent_ref.at[local, rows],
                    sems.at[local * 4 + part],
                )
            )
    for copy in copies:
        copy.start()
    in_even = lax.broadcasted_iota(jnp.int32, (576, LANES), 1) < BLOCK
    for local in range(2):
        request = 2 * chunk + local
        for copy in copies[local * 4 : local * 4 + 4]:
            copy.wait()

        def tile(row, place, local=local):
            start = pl.multiple_of(jnp.maximum(table_ref[row, place], 0) * LANES, LANES)
            return latent_ref[local, :, pl.ds(start, LANES)]

        def fill(places, request=request, local=local, tile=tile):
            for step in range(4):
                row = step * 4 + request
                for place in places:
                    out_ref[local * 4 + step, :, place * LANES : (place + 1) * LANES] = jnp.where(
                        in_even, tile(row, place), tile(row, SLOTS + place)
                    )

        fill(range(4))

        @pl.when(most_of(table_ref, request) > 4)
        def _(fill=fill):
            fill(range(4, SLOTS))


def most_of(table_ref, request):
    most = table_ref[request, 16]
    for step in range(1, 4):
        most = jnp.maximum(most, table_ref[step * 4 + request, 16])
    return most


def gather(chunk, table, latents_t):
    bf16 = jnp.bfloat16
    return call(
        functools.partial(gather_kernel, chunk),
        limit=GATHER_LIMIT,
        in_specs=[pl.BlockSpec(memory_space=pltpu.SMEM), pl.BlockSpec(memory_space=pltpu.HBM)],
        out_shape=jax.ShapeDtypeStruct((PAIRS, 576, SLOTS * LANES), bf16),
        scratch_shapes=[pltpu.VMEM((2, 576, 2048), bf16), pltpu.SemaphoreType.DMA((8,))],
        name="gather_blocks",
    )(table, latents_t)


def attend_kernel(chunk, offsets, table_ref, *refs):
    q_refs = refs[:8]
    block_ref = refs[8]
    own_a, own_b, send_a, send_b, stats_ref, score_ref, weight_ref = refs[9:]
    lane = lax.broadcasted_iota(jnp.int32, (LANES, LANES), 1)
    position = lax.broadcasted_iota(jnp.int32, (1, LANES), 1)
    stats_ref[...] = jnp.zeros((LANES, LANES), jnp.float32)

    def work(local, request, tiles):
        width = tiles * LANES
        for step in range(4):
            row = step * 4 + request
            pair = local * 4 + step
            query = jnp.concatenate(
                [
                    r[at + pair * HEADS : at + (pair + 1) * HEADS, :576]
                    for r, at in zip(q_refs, offsets)
                ],
                axis=0,
            )
            bias = []
            for place in range(tiles):
                at = jnp.where(
                    position < BLOCK, table_ref[row, place], table_ref[row, SLOTS + place]
                )
                usable = (at >= 0) & (at * LANES + position <= table_ref[row, 17])
                bias.append(jnp.where(usable, 0.0, -1e30))
            scores = jnp.dot(
                query, block_ref[pair, :, :width], preferred_element_type=jnp.float32
            )
            score_ref[step, :, :width] = scores * (QK_DIM**-0.5) + jnp.concatenate(bias, axis=1)
        scales = []
        for step in range(4):
            scores = score_ref[step, :, :width]
            peak = jnp.maximum(jnp.max(scores, axis=1, keepdims=True), -1e29)
            weights = jnp.exp(scores - peak)
            total = jnp.maximum(jnp.sum(weights, axis=1, keepdims=True), 1e-30)
            weight_ref[step, :, :width] = weights.astype(jnp.bfloat16)
            scales.append(1.0 / total)
            stats_ref[...] = jnp.where(
                lane == local * 4 + step, peak + jnp.log(total), stats_ref[...]
            )
        for step in range(4):
            mixed = lax.dot_general(
                weight_ref[step, :, :width],
                block_ref[local * 4 + step, :KV, :width],
                (((1,), (1,)), ((), ())),
                preferred_element_type=jnp.float32,
            )
            mixed = (mixed * scales[step]).astype(jnp.bfloat16)
            for across, (out_a, out_b) in enumerate(((own_a, own_b), (send_a, send_b))):
                for out, members in ((out_a, FAR), (out_b, NEAR)):
                    for place, member in enumerate(members):
                        source = (across * 4 + member) * HEADS
                        row = place * ROWS + (local * 4 + step) * HEADS
                        out[row : row + HEADS, :] = mixed[source : source + HEADS]

    for local in range(2):
        request = 2 * chunk + local
        most = most_of(table_ref, request)

        @pl.when(most <= 4)
        def _(local=local, request=request):
            work(local, request, 4)

        @pl.when(most > 4)
        def _(local=local, request=request):
            work(local, request, 8)

    store_stats(send_a, 2 * ROWS, stats_ref[...])


def attend(chunk, table, gathered_queries, blocks):
    bf16 = jnp.bfloat16
    return call(
        functools.partial(attend_kernel, chunk, tuple(at for _, at in gathered_queries)),
        limit=ATTEND_LIMIT,
        in_specs=[pl.BlockSpec(memory_space=pltpu.SMEM)] + [pl.BlockSpec()] * 9,
        out_shape=[
            jax.ShapeDtypeStruct((2 * ROWS, KV), bf16),
            jax.ShapeDtypeStruct((2 * ROWS, KV), bf16),
            jax.ShapeDtypeStruct((2 * ROWS + EXTRA, KV), bf16),
            jax.ShapeDtypeStruct((2 * ROWS, KV), bf16),
            jax.ShapeDtypeStruct((LANES, LANES), jnp.float32),
        ],
        scratch_shapes=[
            pltpu.VMEM((4, LANES, SLOTS * LANES), jnp.float32),
            pltpu.VMEM((4, LANES, SLOTS * LANES), bf16),
        ],
        name="attend",
    )(table, *(array for array, _ in gathered_queries), blocks)


def joined(own_ref, other_ref, place, weight_own, weight_other):
    for pair in range(PAIRS):
        row = place * ROWS + pair * HEADS
        own = own_ref[row : row + HEADS, :].astype(jnp.float32)
        other = other_ref[row : row + HEADS, :].astype(jnp.float32)
        yield pair, (
            own * weight_own[:, pair : pair + 1] + other * weight_other[:, pair : pair + 1]
        )


def weigh(own, other):
    peak = jnp.maximum(own, other)
    own, other = jnp.exp(own - peak), jnp.exp(other - peak)
    total = own + other
    return own / total, other / total, peak + jnp.log(total)


def rows_of(member):
    return slice(member * HEADS, (member + 1) * HEADS)


def join_far_kernel(own_ref, other_ref, stats_ref, out_ref, weight_ref, lse_ref):
    own, other, lse = weigh(stats_ref[:64], load_stats(other_ref, 2 * ROWS)[64:])
    lse = jnp.concatenate([lse, jnp.zeros((64, LANES), jnp.float32)], axis=0)
    weight_ref[0] = own
    weight_ref[1] = other
    lse_ref[...] = lse
    for place, member in enumerate(FAR):
        part = rows_of(member)
        for pair, rows in joined(own_ref, other_ref, place, own[part], other[part]):
            row = place * ROWS + pair * HEADS
            out_ref[row : row + HEADS, :] = rows.astype(jnp.bfloat16)
    store_stats(out_ref, 2 * ROWS, lse)


def join_far(own, other, stats):
    return call(
        join_far_kernel,
        out_shape=[
            jax.ShapeDtypeStruct((2 * ROWS + EXTRA, KV), jnp.bfloat16),
            jax.ShapeDtypeStruct((2, 64, LANES), jnp.float32),
            jax.ShapeDtypeStruct((LANES, LANES), jnp.float32),
        ],
        name="join_far",
    )(own, other, stats)


def join_near_kernel(own_ref, other_ref, weight_ref, out_ref):
    for place, member in enumerate(NEAR):
        part = rows_of(member)
        weights = weight_ref[0, part], weight_ref[1, part]
        for pair, rows in joined(own_ref, other_ref, place, *weights):
            row = place * ROWS + pair * HEADS
            out_ref[row : row + HEADS, :] = rows


def join_near(own, other, weights):
    return call(
        join_near_kernel,
        out_shape=jax.ShapeDtypeStruct((2 * ROWS, KV), jnp.float32),
        name="join_near",
    )(own, other, weights)


def join_line_kernel(own_ref, other_ref, lse_ref, out_ref, mine_ref, stats_ref):
    own = jnp.concatenate([lse_ref[rows_of(member)] for member in NEAR], axis=0)
    theirs = load_stats(other_ref, 2 * ROWS)
    other = jnp.concatenate([theirs[rows_of(member)] for member in FAR], axis=0)
    own, other, lse = weigh(own, other)
    lse = jnp.concatenate([lse, jnp.zeros((LANES - 2 * HEADS, LANES), jnp.float32)], axis=0)
    part = rows_of(1)
    for pair, rows in joined(own_ref, other_ref, 1, own[part], other[part]):
        out_ref[pair * HEADS : (pair + 1) * HEADS, :] = rows.astype(jnp.bfloat16)
    store_stats(out_ref, ROWS, lse)
    part = rows_of(0)
    for pair, rows in joined(own_ref, other_ref, 0, own[part], other[part]):
        mine_ref[pair * HEADS : (pair + 1) * HEADS, :] = rows
    stats_ref[...] = lse


def join_line(own, other, lse):
    return call(
        join_line_kernel,
        out_shape=[
            jax.ShapeDtypeStruct((SENT, KV), jnp.bfloat16),
            jax.ShapeDtypeStruct((ROWS, KV), jnp.float32),
            jax.ShapeDtypeStruct((LANES, LANES), jnp.float32),
        ],
        name="join_line",
    )(own, other, lse)


def finish_kernel(stats_ref, own_ref, other_ref, up_ref, *rest):
    out_ref, rows_ref, lifted_ref = rest[-3:]
    own, other, _ = weigh(stats_ref[:HEADS], load_stats(other_ref, ROWS)[rows_of(1)])
    for pair, rows in joined(own_ref, other_ref, 0, own, other):
        part = slice(pair * HEADS, (pair + 1) * HEADS)
        for tile in range(4):
            rows_ref[tile, part, :] = rows[:, tile * LANES : (tile + 1) * LANES]
    for head in range(HEADS):
        attended = jnp.concatenate(
            [rows_ref[tile, pl.ds(head, PAIRS, stride=HEADS), :] for tile in range(4)], axis=1
        ).astype(jnp.bfloat16)
        lifted_ref[pl.ds(head, PAIRS, stride=HEADS), :] = jnp.dot(
            attended, up_ref[head], preferred_element_type=jnp.float32
        )
    for step in range(4):
        for local in range(2):
            row = (local * 4 + step) * HEADS
            out_ref[step, local] = lifted_ref[row : row + HEADS, :].astype(jnp.bfloat16)


def finish(chunk, stats, own, other, up, before):
    specs = [whole((LANES, LANES)), whole((ROWS, KV)), whole((SENT, KV))]
    specs.append(whole((HEADS, KV, 128)))
    args = [stats, own, other, up]
    aliases = {}
    if before is not None:
        specs.append(pl.BlockSpec(memory_space=pl.ANY))
        args.append(before)
        aliases = {len(args) - 1: 0}
    return call(
        finish_kernel,
        grid=(1,),
        in_specs=specs,
        out_specs=pl.BlockSpec((4, 2, HEADS, 128), lambda _: (0, chunk, 0, 0)),
        out_shape=jax.ShapeDtypeStruct((4, 4, HEADS, 128), jnp.bfloat16),
        scratch_shapes=[
            pltpu.VMEM((4, ROWS, LANES), jnp.float32),
            pltpu.VMEM((ROWS, 128), jnp.float32),
        ],
        input_output_aliases=aliases,
        name="finish",
    )(*args)


def assemble_kernel(_, *refs):
    out_ref = refs[-1]
    own = lax.axis_index("req")
    for relative, ref in enumerate(refs[:-1]):
        start = pl.multiple_of((own ^ relative) * 128, 128)
        out_ref[:, pl.ds(start, 128), :] = ref[...]


def assemble(earlier, pieces):
    return call(
        assemble_kernel,
        in_specs=[pl.BlockSpec(memory_space=pl.ANY)] + [pl.BlockSpec()] * 4,
        out_shape=jax.ShapeDtypeStruct((HEADS, KV, 128), jnp.bfloat16),
        name="assemble_up",
    )(earlier, *pieces)


def index_kernel(offsets, table_ref, *refs):
    arrays = refs[:16]
    key_ref, out_ref = refs[16:]
    request = pl.program_id(0)
    local = request % 2
    lane = lax.broadcasted_iota(jnp.int32, (64, LANES), 1)

    def work(members):
        columns = []
        for r, at in members:
            rows = r[at + ROWS : at + SENT, :LANES].astype(jnp.float32)
            rows = jnp.concatenate([rows, jnp.zeros((LANES - PAIRS, LANES), jnp.float32)], axis=0)
            columns.append(rows.T[:8])
        columns = jnp.concatenate(columns, axis=0)
        query_rows, weight_rows = [], []
        for step in range(4):
            pair = local * 4 + step
            tail = jnp.concatenate(
                [r[pl.ds(at + pl.multiple_of(pair * HEADS, HEADS), HEADS), 512:] for r, at in members],
                axis=0,
            )
            tail = tail.astype(jnp.float32).reshape(8, 2, 8, LANES)
            first = tail[:, 0].reshape(64, LANES)
            second = tail[:, 1].reshape(64, LANES)
            query_rows.append(jnp.concatenate([first[:, 64:], second[:, 64:]], axis=1))
            weight_rows.append(
                jnp.sum(jnp.where(lane == pair, columns, 0.0), axis=1, keepdims=True)
            )
        queries = jnp.concatenate(query_rows, axis=0).astype(jnp.bfloat16)
        for part in range(4):
            at = slice(part * 512, (part + 1) * 512)
            products = lax.dot_general(
                queries,
                key_ref[0, at, :],
                (((1,), (1,)), ((), ())),
                preferred_element_type=jnp.float32,
            )
            position = part * 512 + lax.broadcasted_iota(jnp.int32, (1, 512), 1)
            for step in range(4):
                mine = jnp.maximum(products[step * 64 : (step + 1) * 64], 0.0)
                summed = jnp.sum(mine * weight_rows[step], axis=0, keepdims=True)
                out_ref[step, pl.ds(request, 1), at] = jnp.where(
                    position <= table_ref[step * 4 + request, 17], summed, 0.0
                )

    for chunk in range(CHUNKS):

        @pl.when(request // 2 == chunk)
        def _(members=list(zip(arrays[8 * chunk : 8 * chunk + 8], offsets[8 * chunk : 8 * chunk + 8]))):
            work(members)


def index_rows(table, gathered, index_keys):
    members = [*gathered[0], *gathered[1]]
    return call(
        functools.partial(index_kernel, tuple(at for _, at in members)),
        grid_spec=pltpu.PrefetchScalarGridSpec(
            num_scalar_prefetch=1,
            grid=(4,),
            in_specs=[whole(array.shape) for array, _ in members]
            + [pl.BlockSpec((1, 2048, 128), lambda i, _: (i, 0, 0))],
            out_specs=whole((4, 4, 2048)),
        ),
        out_shape=jax.ShapeDtypeStruct((4, 4, 2048), jnp.float32),
        name="index_scores",
    )(table, *(array for array, _ in members), index_keys)


def fast(
    latents,
    index_keys,
    queries,
    index_queries,
    index_weights,
    value_up_weight,
    selection,
    counts,
    lengths,
):
    def across_x(value):
        return lax.ppermute(value, "ctx", [(i, i ^ 1) for i in range(8)])

    def across_z(value, distance):
        return lax.ppermute(value, "ctx", [(i, i ^ (2 * distance)) for i in range(8)])

    def across_req(value, distance):
        return lax.ppermute(value, "req", [(i, i ^ distance) for i in range(4)])

    own0, own1, both = pack(queries, index_queries, index_weights)
    table = plan(after(selection, own0), counts, lengths)
    latents_t = jnp.transpose(latents, (0, 2, 1))

    x0 = across_x(both)
    z2c0, z1c0 = across_z(own0, 2), across_z(own0, 1)

    round1 = (x0, z2c0, z1c0, table)
    x12 = across_x(pair_up(after(z1c0, *round1), z2c0))
    z3c0 = across_z(after(z2c0, *round1), 1)
    z2c1 = across_z(after(own1, *round1), 2)
    blocks0 = gather(0, after(table, *round1), latents_t)

    round2 = (x12, z3c0, z2c1, blocks0)
    x32 = across_x(pair_up(after(z3c0, *round2), z2c1))
    z1c1 = across_z(after(own1, *round2), 1)
    z3c1 = across_z(after(z2c1, *round2), 1)
    blocks1 = gather(1, after(table, *round2), latents_t)
    up_y = across_req(after(value_up_weight, *round2), 2)

    round3 = (x32, z1c1, z3c1, blocks1)
    last = pair_up(after(z1c1, *round3), z3c1)
    x13 = across_x(last)
    up_core = across_req(after(value_up_weight, *round3), 1)
    up_both = across_req(after(up_y, *round3), 1)
    gathered = [
        [(own0, 0), (z1c0, 0), (z2c0, 0), (z3c0, 0), (x0, 0), (x12, 0), (x12, SENT), (x32, 0)],
        [(own1, 0), (z1c1, 0), (z2c1, 0), (z3c1, 0), (x0, SENT), (x13, 0), (x32, SENT), (x13, SENT)],
    ]

    own_a0, own_b0, send_a0, send_b0, stats0 = attend(
        0, after(table, last), gathered[0], blocks0
    )
    xa0, xb0 = across_x(send_a0), across_x(send_b0)
    own_a1, own_b1, send_a1, send_b1, stats1 = attend(
        1, after(table, stats0), gathered[1], blocks1
    )
    xa1, xb1 = across_x(send_a1), across_x(send_b1)

    far0, weights0, lse0 = join_far(own_a0, after(xa0, stats1), stats0)
    l0 = across_z(far0, 1)
    near0 = join_near(own_b0, xb0, weights0)
    index_scores = index_rows(after(table, far0), gathered, index_keys)
    up = assemble(index_scores, [value_up_weight, up_core, up_y, up_both])

    message0, mine0, stats0 = join_line(near0, l0, lse0)
    f0 = across_z(message0, 2)
    far1, weights1, lse1 = join_far(own_a1, xa1, stats1)
    l1 = across_z(far1, 1)
    near1 = join_near(own_b1, xb1, weights1)
    message1, mine1, stats1 = join_line(near1, l1, lse1)
    f1 = across_z(message1, 2)
    head_values = finish(0, stats0, mine0, f0, up, None)
    head_values = finish(1, stats1, mine1, f1, up, head_values)
    return (head_values, index_scores)


def compact_slots(owned_slot, local_block, capacity):
    ranking = jnp.cumsum(owned_slot.astype(jnp.int32), axis=-1) - 1
    places = jnp.arange(capacity, dtype=jnp.int32)
    chosen = (owned_slot[..., None, :] & (ranking[..., None, :] == places[:, None])).astype(
        jnp.int32
    )
    block_index = jnp.sum(chosen * local_block[..., None, :], axis=-1)
    filled = jnp.sum(chosen, axis=-1) > 0
    return (block_index, filled)


def per_device(
    latents,
    index_keys,
    queries,
    index_queries,
    index_weights,
    value_up_weight,
    selection,
    counts,
    lengths,
):
    own_shard = lax.axis_index("ctx")
    step_count, request_count, slot_count = selection.shape
    half_axis = lax.axis_size("ctx") // 2
    capacity = max(2, (slot_count - 2) // half_axis + 1)
    context_dev = latents.shape[1]
    row_width = latents.shape[2]
    blocks_dev = context_dev // BLOCK
    score_scale = QK_DIM ** (-0.5)
    all_query, all_index_query, all_index_weight = (
        lax.all_gather(queries, "ctx", axis=2, tiled=True),
        lax.all_gather(index_queries, "ctx", axis=2, tiled=True),
        lax.all_gather(index_weights, "ctx", axis=2, tiled=True),
    )
    step_ids = jnp.arange(step_count, dtype=jnp.int32)
    limits = lengths[None, :] + step_ids[:, None]
    token_pos = own_shard * context_dev + jnp.arange(context_dev, dtype=jnp.int32)
    products = jnp.einsum(
        "srhd,rcd->srhc", all_index_query, index_keys, preferred_element_type=jnp.float32
    )
    weighted = jnp.einsum(
        "srhc,srh->src", jnp.maximum(products, 0.0), all_index_weight.astype(jnp.float32)
    )
    index_scores = jnp.where(token_pos[None, None, :] <= limits[:, :, None], weighted, 0.0)
    local_block = selection - own_shard * blocks_dev
    slot_ids = jnp.arange(slot_count, dtype=jnp.int32)
    owned_slot = (
        (local_block >= 0)
        & (local_block < blocks_dev)
        & (slot_ids[None, None, :] < counts[:, :, None])
    )
    block_index, filled = compact_slots(owned_slot, local_block, capacity)
    block_tiles = latents.reshape(request_count, blocks_dev, BLOCK, row_width)
    request_numbers = jnp.arange(request_count, dtype=jnp.int32)[None, :, None]
    gathered = block_tiles[request_numbers, block_index].reshape(
        step_count, request_count, capacity * BLOCK, row_width
    )
    positions = (block_index + own_shard * blocks_dev)[..., None] * BLOCK + jnp.arange(
        BLOCK, dtype=jnp.int32
    )
    usable = filled[..., None] & (positions <= limits[:, :, None, None])
    usable = usable.reshape(step_count, request_count, 1, capacity * BLOCK)
    scores = (
        jnp.einsum("srhl,srtl->srht", all_query, gathered, preferred_element_type=jnp.float32)
        * score_scale
    )
    scores = jnp.where(usable, scores, -1e30)
    peak_score = jnp.max(scores, axis=-1)
    exp_weights = jnp.where(usable, jnp.exp(scores - peak_score[..., None]), 0.0)
    row_total = jnp.sum(exp_weights, axis=-1)
    mixed_rows = jnp.einsum(
        "srht,srtk->srhk",
        exp_weights.astype(jnp.bfloat16),
        gathered[..., :KV],
        preferred_element_type=jnp.float32,
    )
    global_peak = lax.pmax(peak_score, "ctx")
    shrink = jnp.exp(peak_score - global_peak)
    share_total, mixed_share = (
        lax.psum_scatter(
            (row_total * shrink).astype(jnp.bfloat16), "ctx", scatter_dimension=2, tiled=True
        ).astype(jnp.float32),
        lax.psum_scatter(
            (mixed_rows * shrink[..., None]).astype(jnp.bfloat16),
            "ctx",
            scatter_dimension=2,
            tiled=True,
        ).astype(jnp.float32),
    )
    attended_output = (mixed_share / share_total[..., None]).astype(jnp.bfloat16)
    complete_up_matrix = lax.all_gather(value_up_weight, "req", axis=1, tiled=True)
    lifted_values = jnp.einsum(
        "xefy,fym->xefm", attended_output, complete_up_matrix, preferred_element_type=jnp.float32
    )
    head_values = lifted_values.astype(jnp.bfloat16)
    return (head_values, index_scores)


def solution(mesh):
    placed = (
        P("req", "ctx", None),
        P("req", "ctx", None),
        P(None, "req", "ctx", None),
        P(None, "req", "ctx", None),
        P(None, "req", "ctx"),
        P("ctx", "req", None),
        P(None, "req", None),
        P(None, "req"),
        P("req"),
    )
    sizes = dict(mesh.shape)
    plan = fast if (sizes["ctx"], sizes["req"]) == (8, 4) else per_device
    return jax.shard_map(
        plan,
        mesh=mesh,
        in_specs=placed,
        out_specs=(P(None, "req", "ctx", None), P(None, "req", "ctx")),
        check_vma=False,
    )
```

```python
import functools

import jax
import jax.numpy as jnp
from jax import lax
from jax.experimental import pallas as pl
from jax.experimental.pallas import tpu as pltpu
from jax.sharding import PartitionSpec as P

KV = 512
QK_DIM = 192
BLOCK = 64
VMEM_LIMIT = 16 * 1024 * 1024
PACK_LIMIT = 63_000_000
ATTEND_LIMIT = 20 * 1024 * 1024
TABLE = 32
GATHER_LIMIT = (47_000_000, 38_000_000)

CHUNKS = 2
PAIRS = 8
HEADS = 16
ROWS = PAIRS * HEADS
EXTRA = 8
SENT = ROWS + EXTRA
WIDE = 640
SLOTS = 8
LANES = 128


def call(body, limit=VMEM_LIMIT, us=0.3, **kwargs):
    return pl.pallas_call(
        body,
        cost_estimate=pl.CostEstimate(
            flops=int(us * 1e9), bytes_accessed=int(us * 3e6), transcendentals=0
        ),
        compiler_params=pltpu.CompilerParams(vmem_limit_bytes=limit),
        **kwargs,
    )


def after(value, *earlier):
    return lax.optimization_barrier((value, *earlier))[0]


def whole(shape):
    return pl.BlockSpec(shape, lambda *_: (0,) * len(shape))


def pack_kernel(q_hbm, iq_hbm, iw_hbm, out0_ref, out1_ref, both_ref, q_ref, iq_ref, iw_ref, sems):
    small = pltpu.make_async_copy(iw_hbm, iw_ref, sems.at[4])
    small.start()
    copies = []
    for chunk in range(CHUNKS):
        requests = pl.ds(2 * chunk, 2)
        copies.append(
            (
                pltpu.make_async_copy(
                    q_hbm.at[:, requests], q_ref.at[chunk], sems.at[2 * chunk]
                ),
                pltpu.make_async_copy(
                    iq_hbm.at[:, requests], iq_ref.at[chunk], sems.at[2 * chunk + 1]
                ),
            )
        )
        for copy in copies[-1]:
            copy.start()
    small.wait()
    for chunk, out_ref in enumerate((out0_ref, out1_ref)):
        for copy in copies[chunk]:
            copy.wait()
        rows = []
        for local in range(2):
            for step in range(4):
                row = (local * 4 + step) * HEADS
                query = q_ref[chunk, step, local]
                index_query = iq_ref[chunk, step, local]
                halves = jnp.concatenate([index_query[:, :64], index_query[:, 64:]], axis=0)
                out_ref[row : row + HEADS, :512] = query[:, :512]
                out_ref[row : row + HEADS, 512:] = jnp.concatenate(
                    [query[:, 512:], halves], axis=1
                )
                request = 2 * chunk + local
                rows.append(iw_ref[step, request : request + 1, :].astype(jnp.float32))
        weights = jnp.concatenate(rows, axis=0)
        weights = jnp.concatenate([weights, jnp.zeros((PAIRS, LANES - 8), jnp.float32)], axis=1)
        out_ref[ROWS:, :LANES] = weights.astype(jnp.bfloat16)
        out_ref[ROWS:, LANES:] = jnp.zeros((EXTRA, WIDE - LANES), jnp.bfloat16)
        both_ref[chunk * SENT : (chunk + 1) * SENT, :] = out_ref[...]


def pack(queries, index_queries, index_weights):
    bf16 = jnp.bfloat16
    return call(
        pack_kernel,
        limit=PACK_LIMIT,
        in_specs=[pl.BlockSpec(memory_space=pltpu.HBM)] * 3,
        out_shape=[jax.ShapeDtypeStruct((SENT, WIDE), bf16)] * 2
        + [jax.ShapeDtypeStruct((2 * SENT, WIDE), bf16)],
        scratch_shapes=[
            pltpu.VMEM((2, 4, 2, HEADS, 576), bf16),
            pltpu.VMEM((2, 4, 2, 8, 128), bf16),
            pltpu.VMEM((4, 4, 8), bf16),
            pltpu.SemaphoreType.DMA((5,)),
        ],
        name="pack",
        us=2,
    )(queries, index_queries, index_weights)


def pair_up_kernel(first_ref, second_ref, out_ref):
    out_ref[:SENT, :] = first_ref[...]
    out_ref[SENT:, :] = second_ref[...]


def pair_up(first, second):
    return call(
        pair_up_kernel,
        out_shape=jax.ShapeDtypeStruct((2 * SENT, WIDE), jnp.bfloat16),
        name="pair_up",
    )(first, second)


def second_of_kernel(both_ref, out_ref):
    out_ref[...] = both_ref[SENT:, :]


def second_of(both):
    return call(
        second_of_kernel,
        out_shape=jax.ShapeDtypeStruct((SENT, WIDE), jnp.bfloat16),
        name="second_of",
    )(both)


def plan_kernel(selection_ref, counts_ref, lengths_ref, out_ref):
    shard = lax.axis_index("ctx")
    row = lax.broadcasted_iota(jnp.int32, (16, 1), 0)
    count = jnp.zeros((16, 1), jnp.int32)
    limit = jnp.zeros((16, 1), jnp.int32)
    for step in range(4):
        for request in range(4):
            here = row == step * 4 + request
            count = jnp.where(here, counts_ref[step, request], count)
            limit = jnp.where(here, lengths_ref[request] + step - shard * 2048, limit)
    selection = jnp.concatenate([selection_ref[step] for step in range(4)], axis=0)
    local = selection - shard * (2048 // BLOCK)
    slot = lax.broadcasted_iota(jnp.int32, (16, 32), 1)
    owned = (local >= 0) & (local < 2048 // BLOCK) & (slot < count)
    before = (
        lax.broadcasted_iota(jnp.int32, (32, 32), 0) < lax.broadcasted_iota(jnp.int32, (32, 32), 1)
    ).astype(jnp.float32)
    lane = lax.broadcasted_iota(jnp.int32, (16, LANES), 1)
    table = jnp.full((16, LANES), -1, jnp.int32)
    most = jnp.zeros((16, 1), jnp.int32)
    for parity in range(2):
        mine = owned & (local % 2 == parity)
        mine_f = jnp.where(mine, 1.0, 0.0)
        rank = jnp.dot(mine_f, before, preferred_element_type=jnp.float32).astype(jnp.int32)
        for place in range(SLOTS):
            chosen = mine & (rank == place)
            found = jnp.sum(jnp.where(chosen, local // 2 + 1, 0), axis=1, keepdims=True) - 1
            table = jnp.where(lane == parity * SLOTS + place, found, table)
        most = jnp.maximum(most, jnp.sum(mine_f, axis=1, keepdims=True).astype(jnp.int32))
    table = jnp.where(lane == 16, most, table)
    table = jnp.where(lane == 17, limit, table)
    out_ref[...] = table[:, :TABLE]


def plan(selection, counts, lengths):
    smem = pl.BlockSpec(memory_space=pltpu.SMEM)
    return call(
        plan_kernel,
        in_specs=[pl.BlockSpec(), smem, smem],
        out_shape=jax.ShapeDtypeStruct((16, TABLE), jnp.int32),
        name="plan",
        us=0.9,
    )(selection, counts, lengths)


def split3(value):
    high = value.astype(jnp.bfloat16)
    rest = value - high.astype(jnp.float32)
    middle = rest.astype(jnp.bfloat16)
    low = (rest - middle.astype(jnp.float32)).astype(jnp.bfloat16)
    return high, middle, low


def store_stats(out_ref, row, stats):
    turned = stats.T[:PAIRS]
    for place, part in enumerate(split3(turned)):
        out_ref[row : row + PAIRS, place * LANES : (place + 1) * LANES] = part
    out_ref[row : row + PAIRS, 3 * LANES :] = jnp.zeros((PAIRS, LANES), jnp.bfloat16)


def load_stats(in_ref, row):
    parts = [
        in_ref[row : row + PAIRS, place * LANES : (place + 1) * LANES].astype(jnp.float32)
        for place in range(3)
    ]
    turned = (parts[0] + parts[1]) + parts[2]
    return jnp.concatenate([turned, jnp.zeros((LANES - PAIRS, LANES), jnp.float32)], axis=0).T


def gather_kernel(chunk, table_ref, latent_hbm, out_ref, latent_ref, sems):
    copies = []
    for local in range(2):
        for part in range(4):
            rows = pl.ds(part * 144, 144)
            copies.append(
                pltpu.make_async_copy(
                    latent_hbm.at[2 * chunk + local, rows],
                    latent_ref.at[local, rows],
                    sems.at[local * 4 + part],
                )
            )
    for copy in copies:
        copy.start()
    in_even = lax.broadcasted_iota(jnp.int32, (576, LANES), 1) < BLOCK
    for local in range(2):
        request = 2 * chunk + local
        for copy in copies[local * 4 : local * 4 + 4]:
            copy.wait()

        def tile(row, place, local=local):
            start = pl.multiple_of(jnp.maximum(table_ref[row, place], 0) * LANES, LANES)
            return latent_ref[local, :, pl.ds(start, LANES)]

        def fill(places, request=request, local=local, tile=tile):
            for step in range(4):
                row = step * 4 + request
                for place in places:
                    out_ref[local * 4 + step, :, place * LANES : (place + 1) * LANES] = jnp.where(
                        in_even, tile(row, place), tile(row, SLOTS + place)
                    )

        fill(range(4))

        @pl.when(most_of(table_ref, request) > 4)
        def _(fill=fill):
            fill(range(4, SLOTS))


def most_of(table_ref, request):
    most = table_ref[request, 16]
    for step in range(1, 4):
        most = jnp.maximum(most, table_ref[step * 4 + request, 16])
    return most


def gather(chunk, table, latents_t):
    bf16 = jnp.bfloat16
    return call(
        functools.partial(gather_kernel, chunk),
        limit=GATHER_LIMIT[chunk],
        in_specs=[pl.BlockSpec(memory_space=pltpu.SMEM), pl.BlockSpec(memory_space=pltpu.HBM)],
        out_shape=jax.ShapeDtypeStruct((PAIRS, 576, SLOTS * LANES), bf16),
        scratch_shapes=[pltpu.VMEM((2, 576, 2048), bf16), pltpu.SemaphoreType.DMA((8,))],
        name="gather_blocks",
        us=5,
    )(table, latents_t)


def attend_kernel(chunk, offsets, table_ref, *refs):
    q_refs = refs[:8]
    block_ref = refs[8]
    near, far, cross, send_x, send_z, stats_ref, score_ref, weight_ref = refs[9:]
    lane = lax.broadcasted_iota(jnp.int32, (LANES, LANES), 1)
    position = lax.broadcasted_iota(jnp.int32, (1, LANES), 1)
    stats_ref[...] = jnp.zeros((LANES, LANES), jnp.float32)

    def work(local, request, tiles):
        width = tiles * LANES
        for step in range(4):
            row = step * 4 + request
            pair = local * 4 + step
            query = jnp.concatenate(
                [
                    r[at + pair * HEADS : at + (pair + 1) * HEADS, :576]
                    for r, at in zip(q_refs, offsets)
                ],
                axis=0,
            )
            bias = []
            for place in range(tiles):
                at = jnp.where(
                    position < BLOCK, table_ref[row, place], table_ref[row, SLOTS + place]
                )
                usable = (at >= 0) & (at * LANES + position <= table_ref[row, 17])
                bias.append(jnp.where(usable, 0.0, -1e30))
            scores = jnp.dot(
                query, block_ref[pair, :, :width], preferred_element_type=jnp.float32
            )
            score_ref[step, :, :width] = scores * (QK_DIM**-0.5) + jnp.concatenate(bias, axis=1)
        scales = []
        for step in range(4):
            scores = score_ref[step, :, :width]
            peak = jnp.maximum(jnp.max(scores, axis=1, keepdims=True), -1e29)
            weights = jnp.exp(scores - peak)
            total = jnp.maximum(jnp.sum(weights, axis=1, keepdims=True), 1e-30)
            weight_ref[step, :, :width] = weights.astype(jnp.bfloat16)
            scales.append(1.0 / total)
            stats_ref[...] = jnp.where(
                lane == local * 4 + step, peak + jnp.log(total), stats_ref[...]
            )
        for step in range(4):
            mixed = lax.dot_general(
                weight_ref[step, :, :width],
                block_ref[local * 4 + step, :KV, :width],
                (((1,), (1,)), ((), ())),
                preferred_element_type=jnp.float32,
            )
            mixed = (mixed * scales[step]).astype(jnp.bfloat16)
            row = (local * 4 + step) * HEADS
            for out, places in (
                (near, (0, 2)),
                (far, (1, 3)),
                (cross, (4, 6)),
                (send_x, (5,)),
                (send_z, (7,)),
            ):
                for half, place in enumerate(places):
                    at = half * ROWS + row
                    out[at : at + HEADS, :] = mixed[place * HEADS : (place + 1) * HEADS]

    for local in range(2):
        request = 2 * chunk + local
        most = most_of(table_ref, request)

        @pl.when(most <= 4)
        def _(local=local, request=request):
            work(local, request, 4)

        @pl.when(most > 4)
        def _(local=local, request=request):
            work(local, request, 8)

    store_stats(send_x, ROWS, stats_ref[...])
    store_stats(send_z, ROWS, stats_ref[...])


def attend(chunk, table, gathered_queries, blocks):
    bf16 = jnp.bfloat16
    return call(
        functools.partial(attend_kernel, chunk, tuple(at for _, at in gathered_queries)),
        limit=ATTEND_LIMIT,
        in_specs=[pl.BlockSpec(memory_space=pltpu.SMEM)] + [pl.BlockSpec()] * 9,
        out_shape=[
            jax.ShapeDtypeStruct((2 * ROWS, KV), bf16),
            jax.ShapeDtypeStruct((2 * ROWS, KV), bf16),
            jax.ShapeDtypeStruct((2 * ROWS, KV), bf16),
            jax.ShapeDtypeStruct((SENT, KV), bf16),
            jax.ShapeDtypeStruct((SENT, KV), bf16),
            jax.ShapeDtypeStruct((LANES, LANES), jnp.float32),
        ],
        scratch_shapes=[
            pltpu.VMEM((4, LANES, SLOTS * LANES), jnp.float32),
            pltpu.VMEM((4, LANES, SLOTS * LANES), bf16),
        ],
        name="attend",
        us=3.6,
    )(table, *(array for array, _ in gathered_queries), blocks)


def group(number):
    return slice(number * HEADS, (number + 1) * HEADS)


def weigh(*stats):
    peak = functools.reduce(jnp.maximum, stats)
    weights = [jnp.exp(value - peak) for value in stats]
    total = functools.reduce(jnp.add, weights)
    return [value / total for value in weights], peak + jnp.log(total)


def joined(parts, weights):
    for pair in range(PAIRS):
        rows = None
        for (ref, start), weight in zip(parts, weights):
            at = start + pair * HEADS
            part = ref[at : at + HEADS, :].astype(jnp.float32) * weight[:, pair : pair + 1]
            rows = part if rows is None else rows + part
        yield slice(pair * HEADS, (pair + 1) * HEADS), rows


def stack(stats, new):
    return jnp.concatenate([new.get(number, stats[group(number)]) for number in range(8)], axis=0)


def join_cross_kernel(far, cross, from_x, from_z, stats_ref, to_z, to_x, out_stats):
    stats = stats_ref[...]
    weights, lse1 = weigh(stats[group(1)], load_stats(from_x, ROWS)[group(5)])
    for rows, value in joined(((far, 0), (from_x, 0)), weights):
        to_z[rows, :] = value.astype(jnp.bfloat16)
    to_z[ROWS : 2 * ROWS, :] = far[ROWS:, :]
    weights, lse6 = weigh(stats[group(6)], load_stats(from_z, ROWS)[group(7)])
    to_x[:ROWS, :] = cross[:ROWS, :]
    for rows, value in joined(((cross, ROWS), (from_z, 0)), weights):
        to_x[ROWS + rows.start : ROWS + rows.stop, :] = value.astype(jnp.bfloat16)
    stats = stack(stats, {1: lse1, 6: lse6})
    out_stats[...] = stats
    store_stats(to_z, 2 * ROWS, stats)
    store_stats(to_x, 2 * ROWS, stats)


def join_cross(far, cross, from_x, from_z, stats):
    message = jax.ShapeDtypeStruct((2 * ROWS + EXTRA, KV), jnp.bfloat16)
    return call(
        join_cross_kernel,
        out_shape=[message, message, jax.ShapeDtypeStruct((LANES, LANES), jnp.float32)],
        name="join_cross",
    )(far, cross, from_x, from_z, stats)


def join_near_kernel(near, from_x, from_z, stats_ref, to_z2, mine, out_stats):
    stats, stats_x, stats_z = (
        stats_ref[...],
        load_stats(from_x, 2 * ROWS),
        load_stats(from_z, 2 * ROWS),
    )
    weights, lse2 = weigh(stats[group(2)], stats_x[group(6)], stats_z[group(3)])
    for rows, value in joined(((near, ROWS), (from_x, ROWS), (from_z, ROWS)), weights):
        to_z2[rows, :] = value.astype(jnp.bfloat16)
    weights, lse0 = weigh(stats[group(0)], stats_x[group(4)], stats_z[group(1)])
    for rows, value in joined(((near, 0), (from_x, 0), (from_z, 0)), weights):
        mine[rows, :] = value
    stats = stack(stats, {0: lse0, 2: lse2})
    out_stats[...] = stats
    store_stats(to_z2, ROWS, stats)


def join_near(near, from_x, from_z, stats):
    return call(
        join_near_kernel,
        out_shape=[
            jax.ShapeDtypeStruct((SENT, KV), jnp.bfloat16),
            jax.ShapeDtypeStruct((ROWS, KV), jnp.float32),
            jax.ShapeDtypeStruct((LANES, LANES), jnp.float32),
        ],
        name="join_near",
    )(near, from_x, from_z, stats)


def finish_kernel(stats_ref, own_ref, other_ref, up_ref, *rest):
    out_ref, rows_ref, lifted_ref = rest[-3:]
    weights, _ = weigh(stats_ref[group(0)], load_stats(other_ref, ROWS)[group(2)])
    for part, rows in joined(((own_ref, 0), (other_ref, 0)), weights):
        for tile in range(4):
            rows_ref[tile, part, :] = rows[:, tile * LANES : (tile + 1) * LANES]
    for head in range(HEADS):
        attended = jnp.concatenate(
            [rows_ref[tile, pl.ds(head, PAIRS, stride=HEADS), :] for tile in range(4)], axis=1
        ).astype(jnp.bfloat16)
        lifted_ref[pl.ds(head, PAIRS, stride=HEADS), :] = jnp.dot(
            attended, up_ref[head], preferred_element_type=jnp.float32
        )
    for step in range(4):
        for local in range(2):
            row = (local * 4 + step) * HEADS
            out_ref[step, local] = lifted_ref[row : row + HEADS, :].astype(jnp.bfloat16)


def finish(chunk, stats, own, other, up, before):
    specs = [whole((LANES, LANES)), whole((ROWS, KV)), whole((SENT, KV))]
    specs.append(whole((HEADS, KV, 128)))
    args = [stats, own, other, up]
    aliases = {}
    if before is not None:
        specs.append(pl.BlockSpec(memory_space=pl.ANY))
        args.append(before)
        aliases = {len(args) - 1: 0}
    return call(
        finish_kernel,
        grid=(1,),
        in_specs=specs,
        out_specs=pl.BlockSpec((4, 2, HEADS, 128), lambda _: (0, chunk, 0, 0)),
        out_shape=jax.ShapeDtypeStruct((4, 4, HEADS, 128), jnp.bfloat16),
        scratch_shapes=[
            pltpu.VMEM((4, ROWS, LANES), jnp.float32),
            pltpu.VMEM((ROWS, 128), jnp.float32),
        ],
        input_output_aliases=aliases,
        name="finish",
        us=1.2,
    )(*args)


def assemble_kernel(_, *refs):
    out_ref = refs[-1]
    own = lax.axis_index("req")
    for relative, ref in enumerate(refs[:-1]):
        start = pl.multiple_of((own ^ relative) * 128, 128)
        out_ref[:, pl.ds(start, 128), :] = ref[...]


def assemble(earlier, pieces):
    return call(
        assemble_kernel,
        in_specs=[pl.BlockSpec(memory_space=pl.ANY)] + [pl.BlockSpec()] * 4,
        out_shape=jax.ShapeDtypeStruct((HEADS, KV, 128), jnp.bfloat16),
        name="assemble_up",
        us=1.0,
    )(earlier, *pieces)


def index_kernel(offsets, table_ref, *refs):
    arrays = refs[:16]
    key_ref, out_ref = refs[16:]
    request = pl.program_id(0)
    local = request % 2
    lane = lax.broadcasted_iota(jnp.int32, (64, LANES), 1)

    def work(members):
        columns = []
        for r, at in members:
            rows = r[at + ROWS : at + SENT, :LANES].astype(jnp.float32)
            rows = jnp.concatenate([rows, jnp.zeros((LANES - PAIRS, LANES), jnp.float32)], axis=0)
            columns.append(rows.T[:8])
        columns = jnp.concatenate(columns, axis=0)
        query_rows, weight_rows = [], []
        for step in range(4):
            pair = local * 4 + step
            tail = jnp.concatenate(
                [r[pl.ds(at + pl.multiple_of(pair * HEADS, HEADS), HEADS), 512:] for r, at in members],
                axis=0,
            )
            tail = tail.astype(jnp.float32).reshape(8, 2, 8, LANES)
            first = tail[:, 0].reshape(64, LANES)
            second = tail[:, 1].reshape(64, LANES)
            query_rows.append(jnp.concatenate([first[:, 64:], second[:, 64:]], axis=1))
            weight_rows.append(
                jnp.sum(jnp.where(lane == pair, columns, 0.0), axis=1, keepdims=True)
            )
        queries = jnp.concatenate(query_rows, axis=0).astype(jnp.bfloat16)
        for part in range(4):
            at = slice(part * 512, (part + 1) * 512)
            products = lax.dot_general(
                queries,
                key_ref[0, at, :],
                (((1,), (1,)), ((), ())),
                preferred_element_type=jnp.float32,
            )
            position = part * 512 + lax.broadcasted_iota(jnp.int32, (1, 512), 1)
            for step in range(4):
                mine = jnp.maximum(products[step * 64 : (step + 1) * 64], 0.0)
                summed = jnp.sum(mine * weight_rows[step], axis=0, keepdims=True)
                out_ref[step, pl.ds(request, 1), at] = jnp.where(
                    position <= table_ref[step * 4 + request, 17], summed, 0.0
                )

    for chunk in range(CHUNKS):

        @pl.when(request // 2 == chunk)
        def _(members=list(zip(arrays[8 * chunk : 8 * chunk + 8], offsets[8 * chunk : 8 * chunk + 8]))):
            work(members)


def index_rows(table, gathered, index_keys):
    members = [*gathered[0], *gathered[1]]
    return call(
        functools.partial(index_kernel, tuple(at for _, at in members)),
        grid_spec=pltpu.PrefetchScalarGridSpec(
            num_scalar_prefetch=1,
            grid=(4,),
            in_specs=[whole(array.shape) for array, _ in members]
            + [pl.BlockSpec((1, 2048, 128), lambda i, _: (i, 0, 0))],
            out_specs=whole((4, 4, 2048)),
        ),
        out_shape=jax.ShapeDtypeStruct((4, 4, 2048), jnp.float32),
        name="index_scores",
        us=3.5,
    )(table, *(array for array, _ in members), index_keys)


def fast(
    latents,
    index_keys,
    queries,
    index_queries,
    index_weights,
    value_up_weight,
    selection,
    counts,
    lengths,
):
    def across_x(value):
        return lax.ppermute(value, "ctx", [(i, i ^ 1) for i in range(8)])

    def across_z(value, distance):
        return lax.ppermute(value, "ctx", [(i, i ^ (2 * distance)) for i in range(8)])

    def across_req(value, distance):
        return lax.ppermute(value, "req", [(i, i ^ distance) for i in range(4)])

    own0, own1, both = pack(queries, index_queries, index_weights)
    table = plan(after(selection, own0), counts, lengths)
    latents_t = jnp.transpose(latents, (0, 2, 1))

    x0 = across_x(both)
    z2c0, z1c0 = across_z(own0, 2), across_z(own0, 1)

    round1 = (x0, z2c0, z1c0, table)
    x12 = across_x(pair_up(after(z1c0, *round1), z2c0))
    z3c0 = across_z(after(z2c0, *round1), 1)
    z2c1 = across_z(after(own1, *round1), 2)
    blocks0 = gather(0, after(table, *round1), latents_t)

    up_y = across_req(after(value_up_weight, *round1), 2)
    up_core = across_req(after(value_up_weight, *round1), 1)

    round2 = (x12, z3c0, z2c1, blocks0)
    x32 = across_x(pair_up(after(z3c0, *round2), z2c1))
    z1c1 = across_z(after(own1, *round2), 1)
    z3c1 = across_z(after(z2c1, *round2), 1)
    blocks1 = gather(1, after(table, *round2), latents_t)
    up_both = across_req(after(up_y, *round2), 1)

    round3 = (x32, z1c1, z3c1, blocks1)
    xz1c1 = across_x(after(z1c1, *round3))
    xz2c1 = second_of(after(x32, *round3))
    xz3c1 = across_z(xz2c1, 1)
    gathered = [
        [(own0, 0), (z1c0, 0), (z2c0, 0), (z3c0, 0), (x0, 0), (x12, 0), (x12, SENT), (x32, 0)],
        [(own1, 0), (z1c1, 0), (z2c1, 0), (z3c1, 0), (x0, SENT), (xz1c1, 0), (xz2c1, 0), (xz3c1, 0)],
    ]

    near0, far0, cross0, x5, z7, stats0 = attend(0, after(table, xz2c1), gathered[0], blocks0)
    x5, z7 = across_x(x5), across_z(z7, 1)
    up = assemble(stats0, [value_up_weight, up_core, up_y, up_both])
    near1, far1, cross1, x5c1, z7c1, stats1 = attend(1, after(table, up), gathered[1], blocks1)
    x5c1, z7c1 = across_x(x5c1), across_z(z7c1, 1)

    to_z, to_x, stats0 = join_cross(far0, cross0, after(x5, stats1), z7, stats0)
    from_x, from_z = across_x(to_x), across_z(to_z, 1)
    to_z, to_x, stats1 = join_cross(far1, cross1, after(x5c1, stats0), z7c1, stats1)
    from_xc1, from_zc1 = across_x(to_x), across_z(to_z, 1)
    index_scores = index_rows(after(table, stats1), gathered, index_keys)
    message, mine0, stats0 = join_near(near0, from_x, from_z, stats0)
    last0 = across_z(message, 2)
    message, mine1, stats1 = join_near(near1, from_xc1, from_zc1, stats1)
    last1 = across_z(message, 2)
    head_values = finish(0, stats0, mine0, last0, up, None)
    head_values = finish(1, stats1, mine1, last1, up, head_values)
    return (head_values, index_scores)


def compact_slots(owned_slot, local_block, capacity):
    ranking = jnp.cumsum(owned_slot.astype(jnp.int32), axis=-1) - 1
    places = jnp.arange(capacity, dtype=jnp.int32)
    chosen = (owned_slot[..., None, :] & (ranking[..., None, :] == places[:, None])).astype(
        jnp.int32
    )
    block_index = jnp.sum(chosen * local_block[..., None, :], axis=-1)
    filled = jnp.sum(chosen, axis=-1) > 0
    return (block_index, filled)


def per_device(
    latents,
    index_keys,
    queries,
    index_queries,
    index_weights,
    value_up_weight,
    selection,
    counts,
    lengths,
):
    own_shard = lax.axis_index("ctx")
    step_count, request_count, slot_count = selection.shape
    half_axis = lax.axis_size("ctx") // 2
    capacity = max(2, (slot_count - 2) // half_axis + 1)
    context_dev = latents.shape[1]
    row_width = latents.shape[2]
    blocks_dev = context_dev // BLOCK
    score_scale = QK_DIM ** (-0.5)
    all_query, all_index_query, all_index_weight = (
        lax.all_gather(queries, "ctx", axis=2, tiled=True),
        lax.all_gather(index_queries, "ctx", axis=2, tiled=True),
        lax.all_gather(index_weights, "ctx", axis=2, tiled=True),
    )
    step_ids = jnp.arange(step_count, dtype=jnp.int32)
    limits = lengths[None, :] + step_ids[:, None]
    token_pos = own_shard * context_dev + jnp.arange(context_dev, dtype=jnp.int32)
    products = jnp.einsum(
        "srhd,rcd->srhc", all_index_query, index_keys, preferred_element_type=jnp.float32
    )
    weighted = jnp.einsum(
        "srhc,srh->src", jnp.maximum(products, 0.0), all_index_weight.astype(jnp.float32)
    )
    index_scores = jnp.where(token_pos[None, None, :] <= limits[:, :, None], weighted, 0.0)
    local_block = selection - own_shard * blocks_dev
    slot_ids = jnp.arange(slot_count, dtype=jnp.int32)
    owned_slot = (
        (local_block >= 0)
        & (local_block < blocks_dev)
        & (slot_ids[None, None, :] < counts[:, :, None])
    )
    block_index, filled = compact_slots(owned_slot, local_block, capacity)
    block_tiles = latents.reshape(request_count, blocks_dev, BLOCK, row_width)
    request_numbers = jnp.arange(request_count, dtype=jnp.int32)[None, :, None]
    gathered = block_tiles[request_numbers, block_index].reshape(
        step_count, request_count, capacity * BLOCK, row_width
    )
    positions = (block_index + own_shard * blocks_dev)[..., None] * BLOCK + jnp.arange(
        BLOCK, dtype=jnp.int32
    )
    usable = filled[..., None] & (positions <= limits[:, :, None, None])
    usable = usable.reshape(step_count, request_count, 1, capacity * BLOCK)
    scores = (
        jnp.einsum("srhl,srtl->srht", all_query, gathered, preferred_element_type=jnp.float32)
        * score_scale
    )
    scores = jnp.where(usable, scores, -1e30)
    peak_score = jnp.max(scores, axis=-1)
    exp_weights = jnp.where(usable, jnp.exp(scores - peak_score[..., None]), 0.0)
    row_total = jnp.sum(exp_weights, axis=-1)
    mixed_rows = jnp.einsum(
        "srht,srtk->srhk",
        exp_weights.astype(jnp.bfloat16),
        gathered[..., :KV],
        preferred_element_type=jnp.float32,
    )
    global_peak = lax.pmax(peak_score, "ctx")
    shrink = jnp.exp(peak_score - global_peak)
    share_total, mixed_share = (
        lax.psum_scatter(
            (row_total * shrink).astype(jnp.bfloat16), "ctx", scatter_dimension=2, tiled=True
        ).astype(jnp.float32),
        lax.psum_scatter(
            (mixed_rows * shrink[..., None]).astype(jnp.bfloat16),
            "ctx",
            scatter_dimension=2,
            tiled=True,
        ).astype(jnp.float32),
    )
    attended_output = (mixed_share / share_total[..., None]).astype(jnp.bfloat16)
    complete_up_matrix = lax.all_gather(value_up_weight, "req", axis=1, tiled=True)
    lifted_values = jnp.einsum(
        "xefy,fym->xefm", attended_output, complete_up_matrix, preferred_element_type=jnp.float32
    )
    head_values = lifted_values.astype(jnp.bfloat16)
    return (head_values, index_scores)


def solution(mesh):
    placed = (
        P("req", "ctx", None),
        P("req", "ctx", None),
        P(None, "req", "ctx", None),
        P(None, "req", "ctx", None),
        P(None, "req", "ctx"),
        P("ctx", "req", None),
        P(None, "req", None),
        P(None, "req"),
        P("req"),
    )
    sizes = dict(mesh.shape)
    plan_here = fast if (sizes["ctx"], sizes["req"]) == (8, 4) else per_device
    return jax.shard_map(
        plan_here,
        mesh=mesh,
        in_specs=placed,
        out_specs=(P(None, "req", "ctx", None), P(None, "req", "ctx")),
        check_vma=False,
    )
```

```python
import functools

import jax
import jax.numpy as jnp
from jax import lax
from jax.experimental import pallas as pl
from jax.experimental.pallas import tpu as pltpu
from jax.sharding import PartitionSpec as P

KV = 512
QK_DIM = 192
BLOCK = 64
VMEM_LIMIT = 16 * 1024 * 1024
PACK_LIMIT = 63_000_000
ATTEND_LIMIT = 20 * 1024 * 1024
TABLE = 32
GATHER_LIMIT = (47_000_000, 38_000_000)

CHUNKS = 2
PAIRS = 8
HEADS = 16
ROWS = PAIRS * HEADS
EXTRA = 8
SENT = ROWS + EXTRA
WIDE = 640
SLOTS = 8
LANES = 128


def call(body, limit=VMEM_LIMIT, us=0.3, **kwargs):
    return pl.pallas_call(
        body,
        cost_estimate=pl.CostEstimate(
            flops=int(us * 1e9), bytes_accessed=int(us * 3e6), transcendentals=0
        ),
        compiler_params=pltpu.CompilerParams(vmem_limit_bytes=limit),
        **kwargs,
    )


def after(value, *earlier):
    return lax.optimization_barrier((value, *earlier))[0]


def whole(shape):
    return pl.BlockSpec(shape, lambda *_: (0,) * len(shape))


def pack_kernel(q_hbm, iq_hbm, iw_hbm, out0_ref, out1_ref, both_ref, q_ref, iq_ref, iw_ref, sems):
    small = pltpu.make_async_copy(iw_hbm, iw_ref, sems.at[4])
    small.start()
    copies = []
    for chunk in range(CHUNKS):
        requests = pl.ds(2 * chunk, 2)
        copies.append(
            (
                pltpu.make_async_copy(
                    q_hbm.at[:, requests], q_ref.at[chunk], sems.at[2 * chunk]
                ),
                pltpu.make_async_copy(
                    iq_hbm.at[:, requests], iq_ref.at[chunk], sems.at[2 * chunk + 1]
                ),
            )
        )
        for copy in copies[-1]:
            copy.start()
    small.wait()
    for chunk, out_ref in enumerate((out0_ref, out1_ref)):
        for copy in copies[chunk]:
            copy.wait()
        rows = []
        for local in range(2):
            for step in range(4):
                row = (local * 4 + step) * HEADS
                query = q_ref[chunk, step, local]
                index_query = iq_ref[chunk, step, local]
                halves = jnp.concatenate([index_query[:, :64], index_query[:, 64:]], axis=0)
                out_ref[row : row + HEADS, :512] = query[:, :512]
                out_ref[row : row + HEADS, 512:] = jnp.concatenate(
                    [query[:, 512:], halves], axis=1
                )
                request = 2 * chunk + local
                rows.append(iw_ref[step, request : request + 1, :].astype(jnp.float32))
        weights = jnp.concatenate(rows, axis=0)
        weights = jnp.concatenate([weights, jnp.zeros((PAIRS, LANES - 8), jnp.float32)], axis=1)
        out_ref[ROWS:, :LANES] = weights.astype(jnp.bfloat16)
        out_ref[ROWS:, LANES:] = jnp.zeros((EXTRA, WIDE - LANES), jnp.bfloat16)
        both_ref[chunk * SENT : (chunk + 1) * SENT, :] = out_ref[...]


def pack(queries, index_queries, index_weights):
    bf16 = jnp.bfloat16
    return call(
        pack_kernel,
        limit=PACK_LIMIT,
        in_specs=[pl.BlockSpec(memory_space=pltpu.HBM)] * 3,
        out_shape=[jax.ShapeDtypeStruct((SENT, WIDE), bf16)] * 2
        + [jax.ShapeDtypeStruct((2 * SENT, WIDE), bf16)],
        scratch_shapes=[
            pltpu.VMEM((2, 4, 2, HEADS, 576), bf16),
            pltpu.VMEM((2, 4, 2, 8, 128), bf16),
            pltpu.VMEM((4, 4, 8), bf16),
            pltpu.SemaphoreType.DMA((5,)),
        ],
        name="pack",
        us=2,
    )(queries, index_queries, index_weights)


def pair_up_kernel(first_ref, second_ref, out_ref):
    out_ref[:SENT, :] = first_ref[...]
    out_ref[SENT:, :] = second_ref[...]


def pair_up(first, second):
    return call(
        pair_up_kernel,
        out_shape=jax.ShapeDtypeStruct((2 * SENT, WIDE), jnp.bfloat16),
        name="pair_up",
    )(first, second)


def second_of_kernel(both_ref, out_ref):
    out_ref[...] = both_ref[SENT:, :]


def second_of(both):
    return call(
        second_of_kernel,
        out_shape=jax.ShapeDtypeStruct((SENT, WIDE), jnp.bfloat16),
        name="second_of",
    )(both)


def plan_kernel(selection_ref, counts_ref, lengths_ref, out_ref):
    shard = lax.axis_index("ctx")
    row = lax.broadcasted_iota(jnp.int32, (16, 1), 0)
    count = jnp.zeros((16, 1), jnp.int32)
    limit = jnp.zeros((16, 1), jnp.int32)
    for step in range(4):
        for request in range(4):
            here = row == step * 4 + request
            count = jnp.where(here, counts_ref[step, request], count)
            limit = jnp.where(here, lengths_ref[request] + step - shard * 2048, limit)
    selection = jnp.concatenate([selection_ref[step] for step in range(4)], axis=0)
    local = selection - shard * (2048 // BLOCK)
    slot = lax.broadcasted_iota(jnp.int32, (16, 32), 1)
    owned = (local >= 0) & (local < 2048 // BLOCK) & (slot < count)
    before = (
        lax.broadcasted_iota(jnp.int32, (32, 32), 0) < lax.broadcasted_iota(jnp.int32, (32, 32), 1)
    ).astype(jnp.float32)
    lane = lax.broadcasted_iota(jnp.int32, (16, LANES), 1)
    table = jnp.full((16, LANES), -1, jnp.int32)
    most = jnp.zeros((16, 1), jnp.int32)
    for parity in range(2):
        mine = owned & (local % 2 == parity)
        mine_f = jnp.where(mine, 1.0, 0.0)
        rank = jnp.dot(mine_f, before, preferred_element_type=jnp.float32).astype(jnp.int32)
        for place in range(SLOTS):
            chosen = mine & (rank == place)
            found = jnp.sum(jnp.where(chosen, local // 2 + 1, 0), axis=1, keepdims=True) - 1
            table = jnp.where(lane == parity * SLOTS + place, found, table)
        most = jnp.maximum(most, jnp.sum(mine_f, axis=1, keepdims=True).astype(jnp.int32))
    table = jnp.where(lane == 16, most, table)
    table = jnp.where(lane == 17, limit, table)
    out_ref[...] = table[:, :TABLE]


def plan(selection, counts, lengths):
    smem = pl.BlockSpec(memory_space=pltpu.SMEM)
    return call(
        plan_kernel,
        in_specs=[pl.BlockSpec(), smem, smem],
        out_shape=jax.ShapeDtypeStruct((16, TABLE), jnp.int32),
        name="plan",
        us=0.9,
    )(selection, counts, lengths)


def split3(value):
    high = value.astype(jnp.bfloat16)
    rest = value - high.astype(jnp.float32)
    middle = rest.astype(jnp.bfloat16)
    low = (rest - middle.astype(jnp.float32)).astype(jnp.bfloat16)
    return high, middle, low


def store_stats(out_ref, row, stats):
    turned = stats.T[:PAIRS]
    for place, part in enumerate(split3(turned)):
        out_ref[row : row + PAIRS, place * LANES : (place + 1) * LANES] = part
    out_ref[row : row + PAIRS, 3 * LANES :] = jnp.zeros((PAIRS, LANES), jnp.bfloat16)


def load_stats(in_ref, row):
    parts = [
        in_ref[row : row + PAIRS, place * LANES : (place + 1) * LANES].astype(jnp.float32)
        for place in range(3)
    ]
    turned = (parts[0] + parts[1]) + parts[2]
    return jnp.concatenate([turned, jnp.zeros((LANES - PAIRS, LANES), jnp.float32)], axis=0).T


def gather_kernel(chunk, table_ref, latent_hbm, out_ref, latent_ref, sems):
    copies = []
    for local in range(2):
        for part in range(4):
            rows = pl.ds(part * 144, 144)
            copies.append(
                pltpu.make_async_copy(
                    latent_hbm.at[2 * chunk + local, rows],
                    latent_ref.at[local, rows],
                    sems.at[local * 4 + part],
                )
            )
    for copy in copies:
        copy.start()
    in_even = lax.broadcasted_iota(jnp.int32, (576, LANES), 1) < BLOCK
    for local in range(2):
        request = 2 * chunk + local
        for copy in copies[local * 4 : local * 4 + 4]:
            copy.wait()

        def tile(row, place, local=local):
            start = pl.multiple_of(jnp.maximum(table_ref[row, place], 0) * LANES, LANES)
            return latent_ref[local, :, pl.ds(start, LANES)]

        def fill(places, request=request, local=local, tile=tile):
            for step in range(4):
                row = step * 4 + request
                for place in places:
                    out_ref[local * 4 + step, :, place * LANES : (place + 1) * LANES] = jnp.where(
                        in_even, tile(row, place), tile(row, SLOTS + place)
                    )

        fill(range(4))

        @pl.when(most_of(table_ref, request) > 4)
        def _(fill=fill):
            fill(range(4, SLOTS))


def most_of(table_ref, request):
    most = table_ref[request, 16]
    for step in range(1, 4):
        most = jnp.maximum(most, table_ref[step * 4 + request, 16])
    return most


def gather(chunk, table, latents_t):
    bf16 = jnp.bfloat16
    return call(
        functools.partial(gather_kernel, chunk),
        limit=GATHER_LIMIT[chunk],
        in_specs=[pl.BlockSpec(memory_space=pltpu.SMEM), pl.BlockSpec(memory_space=pltpu.HBM)],
        out_shape=jax.ShapeDtypeStruct((PAIRS, 576, SLOTS * LANES), bf16),
        scratch_shapes=[pltpu.VMEM((2, 576, 2048), bf16), pltpu.SemaphoreType.DMA((8,))],
        name="gather_blocks",
        us=5,
    )(table, latents_t)


def attend_kernel(chunk, offsets, table_ref, *refs):
    q_refs = refs[:8]
    block_ref = refs[8]
    near, far, cross, send_x, send_z, stats_ref, score_ref, weight_ref = refs[9:]
    lane = lax.broadcasted_iota(jnp.int32, (LANES, LANES), 1)
    position = lax.broadcasted_iota(jnp.int32, (1, LANES), 1)
    stats_ref[...] = jnp.zeros((LANES, LANES), jnp.float32)

    def work(local, request, tiles):
        width = tiles * LANES
        for step in range(4):
            row = step * 4 + request
            pair = local * 4 + step
            query = jnp.concatenate(
                [
                    r[at + pair * HEADS : at + (pair + 1) * HEADS, :576]
                    for r, at in zip(q_refs, offsets)
                ],
                axis=0,
            )
            bias = []
            for place in range(tiles):
                at = jnp.where(
                    position < BLOCK, table_ref[row, place], table_ref[row, SLOTS + place]
                )
                usable = (at >= 0) & (at * LANES + position <= table_ref[row, 17])
                bias.append(jnp.where(usable, 0.0, -1e30))
            scores = jnp.dot(
                query, block_ref[pair, :, :width], preferred_element_type=jnp.float32
            )
            score_ref[step, :, :width] = scores * (QK_DIM**-0.5) + jnp.concatenate(bias, axis=1)
        scales = []
        for step in range(4):
            scores = score_ref[step, :, :width]
            peak = jnp.maximum(jnp.max(scores, axis=1, keepdims=True), -1e29)
            weights = jnp.exp(scores - peak)
            total = jnp.maximum(jnp.sum(weights, axis=1, keepdims=True), 1e-30)
            weight_ref[step, :, :width] = weights.astype(jnp.bfloat16)
            scales.append(1.0 / total)
            stats_ref[...] = jnp.where(
                lane == local * 4 + step, peak + jnp.log(total), stats_ref[...]
            )
        for step in range(4):
            mixed = lax.dot_general(
                weight_ref[step, :, :width],
                block_ref[local * 4 + step, :KV, :width],
                (((1,), (1,)), ((), ())),
                preferred_element_type=jnp.float32,
            )
            mixed = (mixed * scales[step]).astype(jnp.bfloat16)
            row = (local * 4 + step) * HEADS
            for out, places in (
                (near, (0, 2)),
                (far, (1, 3)),
                (cross, (4, 6)),
                (send_x, (5,)),
                (send_z, (7,)),
            ):
                for half, place in enumerate(places):
                    at = half * ROWS + row
                    out[at : at + HEADS, :] = mixed[place * HEADS : (place + 1) * HEADS]

    for local in range(2):
        request = 2 * chunk + local
        most = most_of(table_ref, request)

        @pl.when(most <= 4)
        def _(local=local, request=request):
            work(local, request, 4)

        @pl.when(most > 4)
        def _(local=local, request=request):
            work(local, request, 8)

    store_stats(send_x, ROWS, stats_ref[...])
    store_stats(send_z, ROWS, stats_ref[...])


def attend(chunk, table, gathered_queries, blocks):
    bf16 = jnp.bfloat16
    return call(
        functools.partial(attend_kernel, chunk, tuple(at for _, at in gathered_queries)),
        limit=ATTEND_LIMIT,
        in_specs=[pl.BlockSpec(memory_space=pltpu.SMEM)] + [pl.BlockSpec()] * 9,
        out_shape=[
            jax.ShapeDtypeStruct((2 * ROWS, KV), bf16),
            jax.ShapeDtypeStruct((2 * ROWS, KV), bf16),
            jax.ShapeDtypeStruct((2 * ROWS, KV), bf16),
            jax.ShapeDtypeStruct((SENT, KV), bf16),
            jax.ShapeDtypeStruct((SENT, KV), bf16),
            jax.ShapeDtypeStruct((LANES, LANES), jnp.float32),
        ],
        scratch_shapes=[
            pltpu.VMEM((4, LANES, SLOTS * LANES), jnp.float32),
            pltpu.VMEM((4, LANES, SLOTS * LANES), bf16),
        ],
        name="attend",
        us=3.6,
    )(table, *(array for array, _ in gathered_queries), blocks)


def group(number):
    return slice(number * HEADS, (number + 1) * HEADS)


def weigh(*stats):
    peak = functools.reduce(jnp.maximum, stats)
    weights = [jnp.exp(value - peak) for value in stats]
    total = functools.reduce(jnp.add, weights)
    return [value / total for value in weights], peak + jnp.log(total)


def joined(parts, weights):
    for pair in range(PAIRS):
        rows = None
        for (ref, start), weight in zip(parts, weights):
            at = start + pair * HEADS
            part = ref[at : at + HEADS, :].astype(jnp.float32) * weight[:, pair : pair + 1]
            rows = part if rows is None else rows + part
        yield slice(pair * HEADS, (pair + 1) * HEADS), rows


def stack(stats, new):
    return jnp.concatenate([new.get(number, stats[group(number)]) for number in range(8)], axis=0)


def join_cross_kernel(far, cross, from_x, from_z, stats_ref, to_z, to_x, out_stats):
    stats = stats_ref[...]
    weights, lse1 = weigh(stats[group(1)], load_stats(from_x, ROWS)[group(5)])
    for rows, value in joined(((far, 0), (from_x, 0)), weights):
        to_z[rows, :] = value.astype(jnp.bfloat16)
    to_z[ROWS : 2 * ROWS, :] = far[ROWS:, :]
    weights, lse6 = weigh(stats[group(6)], load_stats(from_z, ROWS)[group(7)])
    to_x[:ROWS, :] = cross[:ROWS, :]
    for rows, value in joined(((cross, ROWS), (from_z, 0)), weights):
        to_x[ROWS + rows.start : ROWS + rows.stop, :] = value.astype(jnp.bfloat16)
    stats = stack(stats, {1: lse1, 6: lse6})
    out_stats[...] = stats
    store_stats(to_z, 2 * ROWS, stats)
    store_stats(to_x, 2 * ROWS, stats)


def join_cross(far, cross, from_x, from_z, stats):
    message = jax.ShapeDtypeStruct((2 * ROWS + EXTRA, KV), jnp.bfloat16)
    return call(
        join_cross_kernel,
        out_shape=[message, message, jax.ShapeDtypeStruct((LANES, LANES), jnp.float32)],
        name="join_cross",
    )(far, cross, from_x, from_z, stats)


def join_near_kernel(near, from_x, from_z, stats_ref, to_z2, mine, out_stats):
    stats, stats_x, stats_z = (
        stats_ref[...],
        load_stats(from_x, 2 * ROWS),
        load_stats(from_z, 2 * ROWS),
    )
    weights, lse2 = weigh(stats[group(2)], stats_x[group(6)], stats_z[group(3)])
    for rows, value in joined(((near, ROWS), (from_x, ROWS), (from_z, ROWS)), weights):
        to_z2[rows, :] = value.astype(jnp.bfloat16)
    weights, lse0 = weigh(stats[group(0)], stats_x[group(4)], stats_z[group(1)])
    for rows, value in joined(((near, 0), (from_x, 0), (from_z, 0)), weights):
        mine[rows, :] = value
    stats = stack(stats, {0: lse0, 2: lse2})
    out_stats[...] = stats
    store_stats(to_z2, ROWS, stats)


def join_near(near, from_x, from_z, stats):
    return call(
        join_near_kernel,
        out_shape=[
            jax.ShapeDtypeStruct((SENT, KV), jnp.bfloat16),
            jax.ShapeDtypeStruct((ROWS, KV), jnp.float32),
            jax.ShapeDtypeStruct((LANES, LANES), jnp.float32),
        ],
        name="join_near",
    )(near, from_x, from_z, stats)


def finish_kernel(stats_ref, own_ref, other_ref, up_ref, *rest):
    out_ref, rows_ref, lifted_ref = rest[-3:]
    weights, _ = weigh(stats_ref[group(0)], load_stats(other_ref, ROWS)[group(2)])
    for part, rows in joined(((own_ref, 0), (other_ref, 0)), weights):
        for tile in range(4):
            rows_ref[tile, part, :] = rows[:, tile * LANES : (tile + 1) * LANES]
    for head in range(HEADS):
        attended = jnp.concatenate(
            [rows_ref[tile, pl.ds(head, PAIRS, stride=HEADS), :] for tile in range(4)], axis=1
        ).astype(jnp.bfloat16)
        lifted_ref[pl.ds(head, PAIRS, stride=HEADS), :] = jnp.dot(
            attended, up_ref[head], preferred_element_type=jnp.float32
        )
    for step in range(4):
        for local in range(2):
            row = (local * 4 + step) * HEADS
            out_ref[step, local] = lifted_ref[row : row + HEADS, :].astype(jnp.bfloat16)


def finish(chunk, stats, own, other, up, before):
    specs = [whole((LANES, LANES)), whole((ROWS, KV)), whole((SENT, KV))]
    specs.append(whole((HEADS, KV, 128)))
    args = [stats, own, other, up]
    aliases = {}
    if before is not None:
        specs.append(pl.BlockSpec(memory_space=pl.ANY))
        args.append(before)
        aliases = {len(args) - 1: 0}
    return call(
        finish_kernel,
        grid=(1,),
        in_specs=specs,
        out_specs=pl.BlockSpec((4, 2, HEADS, 128), lambda _: (0, chunk, 0, 0)),
        out_shape=jax.ShapeDtypeStruct((4, 4, HEADS, 128), jnp.bfloat16),
        scratch_shapes=[
            pltpu.VMEM((4, ROWS, LANES), jnp.float32),
            pltpu.VMEM((ROWS, 128), jnp.float32),
        ],
        input_output_aliases=aliases,
        name="finish",
        us=1.2,
    )(*args)


def pair_cores_kernel(own_ref, core_ref, out_ref):
    own = lax.axis_index("req") % 2
    out_ref[own] = own_ref[...]
    out_ref[1 - own] = core_ref[...]


def pair_cores(own, core):
    return call(
        pair_cores_kernel,
        out_shape=jax.ShapeDtypeStruct((2, *own.shape), own.dtype),
        name="pair_cores",
    )(own, core)


def assemble_kernel(_, here_ref, there_ref, out_ref):
    row = lax.axis_index("req") // 2
    for core in range(2):
        for place, ref in ((row, here_ref), (1 - row, there_ref)):
            start = pl.multiple_of((2 * place + core) * 128, 128)
            out_ref[:, pl.ds(start, 128), :] = ref[core]


def assemble(earlier, here, there):
    return call(
        assemble_kernel,
        in_specs=[pl.BlockSpec(memory_space=pl.ANY)] + [pl.BlockSpec()] * 2,
        out_shape=jax.ShapeDtypeStruct((HEADS, KV, 128), jnp.bfloat16),
        name="assemble_up",
        us=1.0,
    )(earlier, here, there)


def index_kernel(offsets, table_ref, *refs):
    arrays = refs[:16]
    key_ref, out_ref = refs[16:]
    request = pl.program_id(0)
    local = request % 2
    lane = lax.broadcasted_iota(jnp.int32, (64, LANES), 1)

    def work(members):
        columns = []
        for r, at in members:
            rows = r[at + ROWS : at + SENT, :LANES].astype(jnp.float32)
            rows = jnp.concatenate([rows, jnp.zeros((LANES - PAIRS, LANES), jnp.float32)], axis=0)
            columns.append(rows.T[:8])
        columns = jnp.concatenate(columns, axis=0)
        query_rows, weight_rows = [], []
        for step in range(4):
            pair = local * 4 + step
            tail = jnp.concatenate(
                [r[pl.ds(at + pl.multiple_of(pair * HEADS, HEADS), HEADS), 512:] for r, at in members],
                axis=0,
            )
            tail = tail.astype(jnp.float32).reshape(8, 2, 8, LANES)
            first = tail[:, 0].reshape(64, LANES)
            second = tail[:, 1].reshape(64, LANES)
            query_rows.append(jnp.concatenate([first[:, 64:], second[:, 64:]], axis=1))
            weight_rows.append(
                jnp.sum(jnp.where(lane == pair, columns, 0.0), axis=1, keepdims=True)
            )
        queries = jnp.concatenate(query_rows, axis=0).astype(jnp.bfloat16)
        for part in range(4):
            at = slice(part * 512, (part + 1) * 512)
            products = lax.dot_general(
                queries,
                key_ref[0, at, :],
                (((1,), (1,)), ((), ())),
                preferred_element_type=jnp.float32,
            )
            position = part * 512 + lax.broadcasted_iota(jnp.int32, (1, 512), 1)
            for step in range(4):
                mine = jnp.maximum(products[step * 64 : (step + 1) * 64], 0.0)
                summed = jnp.sum(mine * weight_rows[step], axis=0, keepdims=True)
                out_ref[step, pl.ds(request, 1), at] = jnp.where(
                    position <= table_ref[step * 4 + request, 17], summed, 0.0
                )

    for chunk in range(CHUNKS):

        @pl.when(request // 2 == chunk)
        def _(members=list(zip(arrays[8 * chunk : 8 * chunk + 8], offsets[8 * chunk : 8 * chunk + 8]))):
            work(members)


def index_rows(table, gathered, index_keys):
    members = [*gathered[0], *gathered[1]]
    return call(
        functools.partial(index_kernel, tuple(at for _, at in members)),
        grid_spec=pltpu.PrefetchScalarGridSpec(
            num_scalar_prefetch=1,
            grid=(4,),
            in_specs=[whole(array.shape) for array, _ in members]
            + [pl.BlockSpec((1, 2048, 128), lambda i, _: (i, 0, 0))],
            out_specs=whole((4, 4, 2048)),
        ),
        out_shape=jax.ShapeDtypeStruct((4, 4, 2048), jnp.float32),
        name="index_scores",
        us=3.5,
    )(table, *(array for array, _ in members), index_keys)


def fast(
    latents,
    index_keys,
    queries,
    index_queries,
    index_weights,
    value_up_weight,
    selection,
    counts,
    lengths,
):
    def across_x(value):
        return lax.ppermute(value, "ctx", [(i, i ^ 1) for i in range(8)])

    def across_z(value, distance):
        return lax.ppermute(value, "ctx", [(i, i ^ (2 * distance)) for i in range(8)])

    def across_req(value, distance):
        return lax.ppermute(value, "req", [(i, i ^ distance) for i in range(4)])

    own0, own1, both = pack(queries, index_queries, index_weights)
    table = plan(after(selection, own0), counts, lengths)
    latents_t = jnp.transpose(latents, (0, 2, 1))

    x0 = across_x(both)
    z2c0, z1c0 = across_z(own0, 2), across_z(own0, 1)

    round1 = (x0, z2c0, z1c0, table)
    x12 = across_x(pair_up(after(z1c0, *round1), z2c0))
    z3c0 = across_z(after(z2c0, *round1), 1)
    z2c1 = across_z(after(own1, *round1), 2)
    blocks0 = gather(0, after(table, *round1), latents_t)

    up_core = across_req(after(value_up_weight, *round1), 1)

    round2 = (x12, z3c0, z2c1, blocks0)
    x32 = across_x(pair_up(after(z3c0, *round2), z2c1))
    z1c1 = across_z(after(own1, *round2), 1)
    z3c1 = across_z(after(z2c1, *round2), 1)
    blocks1 = gather(1, after(table, *round2), latents_t)
    up_here = pair_cores(after(value_up_weight, *round2), up_core)
    up_there = across_req(up_here, 2)

    round3 = (x32, z1c1, z3c1, blocks1)
    xz1c1 = across_x(after(z1c1, *round3))
    xz2c1 = second_of(after(x32, *round3))
    xz3c1 = across_z(xz2c1, 1)
    gathered = [
        [(own0, 0), (z1c0, 0), (z2c0, 0), (z3c0, 0), (x0, 0), (x12, 0), (x12, SENT), (x32, 0)],
        [(own1, 0), (z1c1, 0), (z2c1, 0), (z3c1, 0), (x0, SENT), (xz1c1, 0), (xz2c1, 0), (xz3c1, 0)],
    ]

    near0, far0, cross0, x5, z7, stats0 = attend(0, after(table, xz2c1), gathered[0], blocks0)
    x5, z7 = across_x(x5), across_z(z7, 1)
    near1, far1, cross1, x5c1, z7c1, stats1 = attend(1, after(table, stats0), gathered[1], blocks1)
    x5c1, z7c1 = across_x(x5c1), across_z(z7c1, 1)

    to_z, to_x, stats0 = join_cross(far0, cross0, after(x5, stats1), z7, stats0)
    from_x, from_z = across_x(to_x), across_z(to_z, 1)
    to_z, to_x, stats1 = join_cross(far1, cross1, after(x5c1, stats0), z7c1, stats1)
    from_xc1, from_zc1 = across_x(to_x), across_z(to_z, 1)
    index_scores = index_rows(after(table, stats1), gathered, index_keys)
    up = assemble(index_scores, up_here, up_there)
    message, mine0, stats0 = join_near(after(near0, index_scores), from_x, from_z, stats0)
    last0 = across_z(message, 2)
    message, mine1, stats1 = join_near(near1, from_xc1, from_zc1, stats1)
    last1 = across_z(message, 2)
    head_values = finish(0, stats0, mine0, last0, up, None)
    head_values = finish(1, stats1, mine1, last1, up, head_values)
    return (head_values, index_scores)


def compact_slots(owned_slot, local_block, capacity):
    ranking = jnp.cumsum(owned_slot.astype(jnp.int32), axis=-1) - 1
    places = jnp.arange(capacity, dtype=jnp.int32)
    chosen = (owned_slot[..., None, :] & (ranking[..., None, :] == places[:, None])).astype(
        jnp.int32
    )
    block_index = jnp.sum(chosen * local_block[..., None, :], axis=-1)
    filled = jnp.sum(chosen, axis=-1) > 0
    return (block_index, filled)


def per_device(
    latents,
    index_keys,
    queries,
    index_queries,
    index_weights,
    value_up_weight,
    selection,
    counts,
    lengths,
):
    own_shard = lax.axis_index("ctx")
    step_count, request_count, slot_count = selection.shape
    half_axis = lax.axis_size("ctx") // 2
    capacity = max(2, (slot_count - 2) // half_axis + 1)
    context_dev = latents.shape[1]
    row_width = latents.shape[2]
    blocks_dev = context_dev // BLOCK
    score_scale = QK_DIM ** (-0.5)
    all_query, all_index_query, all_index_weight = (
        lax.all_gather(queries, "ctx", axis=2, tiled=True),
        lax.all_gather(index_queries, "ctx", axis=2, tiled=True),
        lax.all_gather(index_weights, "ctx", axis=2, tiled=True),
    )
    step_ids = jnp.arange(step_count, dtype=jnp.int32)
    limits = lengths[None, :] + step_ids[:, None]
    token_pos = own_shard * context_dev + jnp.arange(context_dev, dtype=jnp.int32)
    products = jnp.einsum(
        "srhd,rcd->srhc", all_index_query, index_keys, preferred_element_type=jnp.float32
    )
    weighted = jnp.einsum(
        "srhc,srh->src", jnp.maximum(products, 0.0), all_index_weight.astype(jnp.float32)
    )
    index_scores = jnp.where(token_pos[None, None, :] <= limits[:, :, None], weighted, 0.0)
    local_block = selection - own_shard * blocks_dev
    slot_ids = jnp.arange(slot_count, dtype=jnp.int32)
    owned_slot = (
        (local_block >= 0)
        & (local_block < blocks_dev)
        & (slot_ids[None, None, :] < counts[:, :, None])
    )
    block_index, filled = compact_slots(owned_slot, local_block, capacity)
    block_tiles = latents.reshape(request_count, blocks_dev, BLOCK, row_width)
    request_numbers = jnp.arange(request_count, dtype=jnp.int32)[None, :, None]
    gathered = block_tiles[request_numbers, block_index].reshape(
        step_count, request_count, capacity * BLOCK, row_width
    )
    positions = (block_index + own_shard * blocks_dev)[..., None] * BLOCK + jnp.arange(
        BLOCK, dtype=jnp.int32
    )
    usable = filled[..., None] & (positions <= limits[:, :, None, None])
    usable = usable.reshape(step_count, request_count, 1, capacity * BLOCK)
    scores = (
        jnp.einsum("srhl,srtl->srht", all_query, gathered, preferred_element_type=jnp.float32)
        * score_scale
    )
    scores = jnp.where(usable, scores, -1e30)
    peak_score = jnp.max(scores, axis=-1)
    exp_weights = jnp.where(usable, jnp.exp(scores - peak_score[..., None]), 0.0)
    row_total = jnp.sum(exp_weights, axis=-1)
    mixed_rows = jnp.einsum(
        "srht,srtk->srhk",
        exp_weights.astype(jnp.bfloat16),
        gathered[..., :KV],
        preferred_element_type=jnp.float32,
    )
    global_peak = lax.pmax(peak_score, "ctx")
    shrink = jnp.exp(peak_score - global_peak)
    share_total, mixed_share = (
        lax.psum_scatter(
            (row_total * shrink).astype(jnp.bfloat16), "ctx", scatter_dimension=2, tiled=True
        ).astype(jnp.float32),
        lax.psum_scatter(
            (mixed_rows * shrink[..., None]).astype(jnp.bfloat16),
            "ctx",
            scatter_dimension=2,
            tiled=True,
        ).astype(jnp.float32),
    )
    attended_output = (mixed_share / share_total[..., None]).astype(jnp.bfloat16)
    complete_up_matrix = lax.all_gather(value_up_weight, "req", axis=1, tiled=True)
    lifted_values = jnp.einsum(
        "xefy,fym->xefm", attended_output, complete_up_matrix, preferred_element_type=jnp.float32
    )
    head_values = lifted_values.astype(jnp.bfloat16)
    return (head_values, index_scores)


def solution(mesh):
    placed = (
        P("req", "ctx", None),
        P("req", "ctx", None),
        P(None, "req", "ctx", None),
        P(None, "req", "ctx", None),
        P(None, "req", "ctx"),
        P("ctx", "req", None),
        P(None, "req", None),
        P(None, "req"),
        P("req"),
    )
    sizes = dict(mesh.shape)
    plan_here = fast if (sizes["ctx"], sizes["req"]) == (8, 4) else per_device
    return jax.shard_map(
        plan_here,
        mesh=mesh,
        in_specs=placed,
        out_specs=(P(None, "req", "ctx", None), P(None, "req", "ctx")),
        check_vma=False,
    )
```

```python
import functools

import jax
import jax.numpy as jnp
from jax import lax
from jax.experimental import pallas as pl
from jax.experimental.pallas import tpu as pltpu
from jax.sharding import PartitionSpec as P

KV = 512
QK_DIM = 192
BLOCK = 64
VMEM_LIMIT = 16 * 1024 * 1024
PACK_LIMIT = 63_000_000
ATTEND_LIMIT = 30_000_000
TABLE = 32
GATHER_LIMIT = (46_000_000, 38_000_000)
SHORT = 4

CHUNKS = 2
PAIRS = 8
HEADS = 16
ROWS = PAIRS * HEADS
EXTRA = 8
SENT = ROWS + EXTRA
WIDE = 640
SLOTS = 8
LANES = 128


def call(body, limit=VMEM_LIMIT, us=0.3, **kwargs):
    return pl.pallas_call(
        body,
        cost_estimate=pl.CostEstimate(
            flops=int(us * 1e9), bytes_accessed=int(us * 3e6), transcendentals=0
        ),
        compiler_params=pltpu.CompilerParams(vmem_limit_bytes=limit),
        **kwargs,
    )


def after(value, *earlier):
    return lax.optimization_barrier((value, *earlier))[0]


def whole(shape):
    return pl.BlockSpec(shape, lambda *_: (0,) * len(shape))


def pack_kernel(q_hbm, iq_hbm, iw_hbm, out0_ref, out1_ref, both_ref, q_ref, iq_ref, iw_ref, sems):
    small = pltpu.make_async_copy(iw_hbm, iw_ref, sems.at[4])
    small.start()
    copies = []
    for chunk in range(CHUNKS):
        requests = pl.ds(2 * chunk, 2)
        copies.append(
            (
                pltpu.make_async_copy(
                    q_hbm.at[:, requests], q_ref.at[chunk], sems.at[2 * chunk]
                ),
                pltpu.make_async_copy(
                    iq_hbm.at[:, requests], iq_ref.at[chunk], sems.at[2 * chunk + 1]
                ),
            )
        )
        for copy in copies[-1]:
            copy.start()
    small.wait()
    for chunk, out_ref in enumerate((out0_ref, out1_ref)):
        for copy in copies[chunk]:
            copy.wait()
        rows = []
        for local in range(2):
            for step in range(4):
                row = (local * 4 + step) * HEADS
                query = q_ref[chunk, step, local]
                index_query = iq_ref[chunk, step, local]
                halves = jnp.concatenate([index_query[:, :64], index_query[:, 64:]], axis=0)
                out_ref[row : row + HEADS, :512] = query[:, :512]
                out_ref[row : row + HEADS, 512:] = jnp.concatenate(
                    [query[:, 512:], halves], axis=1
                )
                request = 2 * chunk + local
                rows.append(iw_ref[step, request : request + 1, :].astype(jnp.float32))
        weights = jnp.concatenate(rows, axis=0)
        weights = jnp.concatenate([weights, jnp.zeros((PAIRS, LANES - 8), jnp.float32)], axis=1)
        out_ref[ROWS:, :LANES] = weights.astype(jnp.bfloat16)
        out_ref[ROWS:, LANES:] = jnp.zeros((EXTRA, WIDE - LANES), jnp.bfloat16)
        both_ref[chunk * SENT : (chunk + 1) * SENT, :] = out_ref[...]


def pack(queries, index_queries, index_weights):
    bf16 = jnp.bfloat16
    return call(
        pack_kernel,
        limit=PACK_LIMIT,
        in_specs=[pl.BlockSpec(memory_space=pltpu.HBM)] * 3,
        out_shape=[jax.ShapeDtypeStruct((SENT, WIDE), bf16)] * 2
        + [jax.ShapeDtypeStruct((2 * SENT, WIDE), bf16)],
        scratch_shapes=[
            pltpu.VMEM((2, 4, 2, HEADS, 576), bf16),
            pltpu.VMEM((2, 4, 2, 8, 128), bf16),
            pltpu.VMEM((4, 4, 8), bf16),
            pltpu.SemaphoreType.DMA((5,)),
        ],
        name="pack",
        us=2,
    )(queries, index_queries, index_weights)


def pair_up_kernel(first_ref, second_ref, out_ref):
    out_ref[:SENT, :] = first_ref[...]
    out_ref[SENT:, :] = second_ref[...]


def pair_up(first, second):
    return call(
        pair_up_kernel,
        out_shape=jax.ShapeDtypeStruct((2 * SENT, WIDE), jnp.bfloat16),
        name="pair_up",
    )(first, second)


def second_of_kernel(both_ref, out_ref):
    out_ref[...] = both_ref[SENT:, :]


def second_of(both):
    return call(
        second_of_kernel,
        out_shape=jax.ShapeDtypeStruct((SENT, WIDE), jnp.bfloat16),
        name="second_of",
    )(both)


def plan_kernel(selection_ref, counts_ref, lengths_ref, out_ref):
    shard = lax.axis_index("ctx")
    row = lax.broadcasted_iota(jnp.int32, (16, 1), 0)
    count = jnp.zeros((16, 1), jnp.int32)
    limit = jnp.zeros((16, 1), jnp.int32)
    for step in range(4):
        for request in range(4):
            here = row == step * 4 + request
            count = jnp.where(here, counts_ref[step, request], count)
            limit = jnp.where(here, lengths_ref[request] + step - shard * 2048, limit)
    selection = jnp.concatenate([selection_ref[step] for step in range(4)], axis=0)
    local = selection - shard * (2048 // BLOCK)
    slot = lax.broadcasted_iota(jnp.int32, (16, 32), 1)
    owned = (local >= 0) & (local < 2048 // BLOCK) & (slot < count)
    before = (
        lax.broadcasted_iota(jnp.int32, (32, 32), 0) < lax.broadcasted_iota(jnp.int32, (32, 32), 1)
    ).astype(jnp.float32)
    lane = lax.broadcasted_iota(jnp.int32, (16, LANES), 1)
    table = jnp.full((16, LANES), -1, jnp.int32)
    most = jnp.zeros((16, 1), jnp.int32)
    for parity in range(2):
        mine = owned & (local % 2 == parity)
        mine_f = jnp.where(mine, 1.0, 0.0)
        rank = jnp.dot(mine_f, before, preferred_element_type=jnp.float32).astype(jnp.int32)
        for place in range(SLOTS):
            chosen = mine & (rank == place)
            found = jnp.sum(jnp.where(chosen, local // 2 + 1, 0), axis=1, keepdims=True) - 1
            table = jnp.where(lane == parity * SLOTS + place, found, table)
        most = jnp.maximum(most, jnp.sum(mine_f, axis=1, keepdims=True).astype(jnp.int32))
    table = jnp.where(lane == 16, most, table)
    table = jnp.where(lane == 17, limit, table)
    out_ref[...] = table[:, :TABLE]


def plan(selection, counts, lengths):
    smem = pl.BlockSpec(memory_space=pltpu.SMEM)
    return call(
        plan_kernel,
        in_specs=[pl.BlockSpec(), smem, smem],
        out_shape=jax.ShapeDtypeStruct((16, TABLE), jnp.int32),
        name="plan",
        us=0.9,
    )(selection, counts, lengths)


def split3(value):
    high = value.astype(jnp.bfloat16)
    rest = value - high.astype(jnp.float32)
    middle = rest.astype(jnp.bfloat16)
    low = (rest - middle.astype(jnp.float32)).astype(jnp.bfloat16)
    return high, middle, low


def store_stats(out_ref, row, stats):
    turned = stats.T[:PAIRS]
    for place, part in enumerate(split3(turned)):
        out_ref[row : row + PAIRS, place * LANES : (place + 1) * LANES] = part
    out_ref[row : row + PAIRS, 3 * LANES :] = jnp.zeros((PAIRS, LANES), jnp.bfloat16)


def load_stats(in_ref, row):
    parts = [
        in_ref[row : row + PAIRS, place * LANES : (place + 1) * LANES].astype(jnp.float32)
        for place in range(3)
    ]
    turned = (parts[0] + parts[1]) + parts[2]
    return jnp.concatenate([turned, jnp.zeros((LANES - PAIRS, LANES), jnp.float32)], axis=0).T


def gather_kernel(requests, table_ref, latent_hbm, out_ref, latent_ref, sems):
    copies = []
    for local, request in enumerate(requests):
        for part in range(4):
            rows = pl.ds(part * 144, 144)
            copies.append(
                pltpu.make_async_copy(
                    latent_hbm.at[request, rows],
                    latent_ref.at[local, rows],
                    sems.at[local * 4 + part],
                )
            )
    for copy in copies:
        copy.start()
    in_even = lax.broadcasted_iota(jnp.int32, (144, LANES), 1) < BLOCK
    for index, copy in enumerate(copies):
        copy.wait()
        local, part = divmod(index, 4)
        request = requests[local]
        rows = slice(part * 144, (part + 1) * 144)

        def tile(row, place, local=local, rows=rows):
            start = pl.multiple_of(jnp.maximum(table_ref[row, place], 0) * LANES, LANES)
            return latent_ref[local, rows, pl.ds(start, LANES)]

        def fill(places, local=local, request=request, rows=rows, tile=tile):
            for step in range(4):
                row = step * 4 + request
                for place in places:
                    out_ref[local * 4 + step, rows, place * LANES : (place + 1) * LANES] = jnp.where(
                        in_even, tile(row, place), tile(row, SLOTS + place)
                    )

        fill(range(SHORT))


def most_of(table_ref, request):
    most = table_ref[request, 16]
    for step in range(1, 4):
        most = jnp.maximum(most, table_ref[step * 4 + request, 16])
    return most


def gather(requests, limit, table, latents_t):
    bf16 = jnp.bfloat16
    count = len(requests)
    return call(
        functools.partial(gather_kernel, requests),
        limit=limit,
        in_specs=[pl.BlockSpec(memory_space=pltpu.SMEM), pl.BlockSpec(memory_space=pltpu.HBM)],
        out_shape=jax.ShapeDtypeStruct((4 * count, 576, SHORT * LANES), bf16),
        scratch_shapes=[
            pltpu.VMEM((count, 576, 2048), bf16),
            pltpu.SemaphoreType.DMA((4 * count,)),
        ],
        name="gather_blocks",
        us=2.6 * count,
    )(table, latents_t)


def attend_kernel(chunk, offsets, table_ref, *refs):
    q_refs = refs[:8]
    block_ref, latent_hbm = refs[8:10]
    near, far, cross, send_x, send_z, stats_ref = refs[10:16]
    score_ref, weight_ref, latent_ref, wide_ref, sem = refs[16:]
    lane = lax.broadcasted_iota(jnp.int32, (LANES, LANES), 1)
    position = lax.broadcasted_iota(jnp.int32, (1, LANES), 1)
    stats_ref[...] = jnp.zeros((LANES, LANES), jnp.float32)

    def query_of(pair):
        return jnp.concatenate(
            [r[at + pair * HEADS : at + (pair + 1) * HEADS, :576] for r, at in zip(q_refs, offsets)],
            axis=0,
        )

    def scores_of(pair, row, blocks, tiles):
        bias = []
        for place in range(tiles):
            at = jnp.where(position < BLOCK, table_ref[row, place], table_ref[row, SLOTS + place])
            usable = (at >= 0) & (at * LANES + position <= table_ref[row, 17])
            bias.append(jnp.where(usable, 0.0, -1e30))
        scores = jnp.dot(query_of(pair), blocks, preferred_element_type=jnp.float32)
        return scores * (QK_DIM**-0.5) + jnp.concatenate(bias, axis=1)

    def weights_of(pair, scores):
        peak = jnp.maximum(jnp.max(scores, axis=1, keepdims=True), -1e29)
        weights = jnp.exp(scores - peak)
        total = jnp.maximum(jnp.sum(weights, axis=1, keepdims=True), 1e-30)
        stats_ref[...] = jnp.where(lane == pair, peak + jnp.log(total), stats_ref[...])
        return weights.astype(jnp.bfloat16), 1.0 / total

    def mix(pair, weights, blocks, scale):
        mixed = lax.dot_general(
            weights, blocks, (((1,), (1,)), ((), ())), preferred_element_type=jnp.float32
        )
        mixed = (mixed * scale).astype(jnp.bfloat16)
        row = pair * HEADS
        for out, places in (
            (near, (0, 2)),
            (far, (1, 3)),
            (cross, (4, 6)),
            (send_x, (5,)),
            (send_z, (7,)),
        ):
            for half, place in enumerate(places):
                at = half * ROWS + row
                out[at : at + HEADS, :] = mixed[place * HEADS : (place + 1) * HEADS]

    def short(local, request):
        for step in range(4):
            pair = local * 4 + step
            score_ref[step] = scores_of(pair, step * 4 + request, block_ref[pair], SHORT)
        scales = []
        for step in range(4):
            weight_ref[step], scale = weights_of(local * 4 + step, score_ref[step])
            scales.append(scale)
        for step in range(4):
            pair = local * 4 + step
            mix(pair, weight_ref[step], block_ref[pair, :KV], scales[step])

    def long(local, request):
        copy = pltpu.make_async_copy(latent_hbm.at[request], latent_ref, sem.at[0])
        copy.start()
        copy.wait()
        in_even = lax.broadcasted_iota(jnp.int32, (576, LANES), 1) < BLOCK
        for step in range(4):
            pair, row = local * 4 + step, step * 4 + request

            def tile(place, row=row):
                start = pl.multiple_of(jnp.maximum(table_ref[row, place], 0) * LANES, LANES)
                return latent_ref[:, pl.ds(start, LANES)]

            for place in range(SLOTS):
                wide_ref[:, place * LANES : (place + 1) * LANES] = jnp.where(
                    in_even, tile(place), tile(SLOTS + place)
                )
            weights, scale = weights_of(pair, scores_of(pair, row, wide_ref[...], SLOTS))
            mix(pair, weights, wide_ref[:KV], scale)

    for local in range(2):
        request = 2 * chunk + local
        most = most_of(table_ref, request)

        @pl.when(most <= SHORT)
        def _(local=local, request=request):
            short(local, request)

        @pl.when(most > SHORT)
        def _(local=local, request=request):
            long(local, request)

    store_stats(send_x, ROWS, stats_ref[...])
    store_stats(send_z, ROWS, stats_ref[...])


def attend(chunk, table, gathered_queries, blocks, latents_t):
    bf16 = jnp.bfloat16
    return call(
        functools.partial(attend_kernel, chunk, tuple(at for _, at in gathered_queries)),
        limit=ATTEND_LIMIT,
        in_specs=[pl.BlockSpec(memory_space=pltpu.SMEM)] + [pl.BlockSpec()] * 9
        + [pl.BlockSpec(memory_space=pltpu.HBM)],
        out_shape=[
            jax.ShapeDtypeStruct((2 * ROWS, KV), bf16),
            jax.ShapeDtypeStruct((2 * ROWS, KV), bf16),
            jax.ShapeDtypeStruct((2 * ROWS, KV), bf16),
            jax.ShapeDtypeStruct((SENT, KV), bf16),
            jax.ShapeDtypeStruct((SENT, KV), bf16),
            jax.ShapeDtypeStruct((LANES, LANES), jnp.float32),
        ],
        scratch_shapes=[
            pltpu.VMEM((4, LANES, SHORT * LANES), jnp.float32),
            pltpu.VMEM((4, LANES, SHORT * LANES), bf16),
            pltpu.VMEM((576, 2048), bf16),
            pltpu.VMEM((576, SLOTS * LANES), bf16),
            pltpu.SemaphoreType.DMA((1,)),
        ],
        name="attend",
        us=3.6,
    )(table, *(array for array, _ in gathered_queries), blocks, latents_t)


def group(number):
    return slice(number * HEADS, (number + 1) * HEADS)


def weigh(*stats):
    peak = functools.reduce(jnp.maximum, stats)
    weights = [jnp.exp(value - peak) for value in stats]
    total = functools.reduce(jnp.add, weights)
    return [value / total for value in weights], peak + jnp.log(total)


def joined(parts, weights):
    for pair in range(PAIRS):
        rows = None
        for (ref, start), weight in zip(parts, weights):
            at = start + pair * HEADS
            part = ref[at : at + HEADS, :].astype(jnp.float32) * weight[:, pair : pair + 1]
            rows = part if rows is None else rows + part
        yield slice(pair * HEADS, (pair + 1) * HEADS), rows


def stack(stats, new):
    return jnp.concatenate([new.get(number, stats[group(number)]) for number in range(8)], axis=0)


def join_cross_kernel(far, cross, from_x, from_z, stats_ref, to_z, to_x, out_stats):
    stats = stats_ref[...]
    weights, lse1 = weigh(stats[group(1)], load_stats(from_x, ROWS)[group(5)])
    for rows, value in joined(((far, 0), (from_x, 0)), weights):
        to_z[rows, :] = value.astype(jnp.bfloat16)
    to_z[ROWS : 2 * ROWS, :] = far[ROWS:, :]
    weights, lse6 = weigh(stats[group(6)], load_stats(from_z, ROWS)[group(7)])
    to_x[:ROWS, :] = cross[:ROWS, :]
    for rows, value in joined(((cross, ROWS), (from_z, 0)), weights):
        to_x[ROWS + rows.start : ROWS + rows.stop, :] = value.astype(jnp.bfloat16)
    stats = stack(stats, {1: lse1, 6: lse6})
    out_stats[...] = stats
    store_stats(to_z, 2 * ROWS, stats)
    store_stats(to_x, 2 * ROWS, stats)


def join_cross(far, cross, from_x, from_z, stats):
    message = jax.ShapeDtypeStruct((2 * ROWS + EXTRA, KV), jnp.bfloat16)
    return call(
        join_cross_kernel,
        out_shape=[message, message, jax.ShapeDtypeStruct((LANES, LANES), jnp.float32)],
        name="join_cross",
    )(far, cross, from_x, from_z, stats)


def join_near_kernel(near, from_x, from_z, stats_ref, to_z2, mine, out_stats):
    stats, stats_x, stats_z = (
        stats_ref[...],
        load_stats(from_x, 2 * ROWS),
        load_stats(from_z, 2 * ROWS),
    )
    weights, lse2 = weigh(stats[group(2)], stats_x[group(6)], stats_z[group(3)])
    for rows, value in joined(((near, ROWS), (from_x, ROWS), (from_z, ROWS)), weights):
        to_z2[rows, :] = value.astype(jnp.bfloat16)
    weights, lse0 = weigh(stats[group(0)], stats_x[group(4)], stats_z[group(1)])
    for rows, value in joined(((near, 0), (from_x, 0), (from_z, 0)), weights):
        mine[rows, :] = value
    stats = stack(stats, {0: lse0, 2: lse2})
    out_stats[...] = stats
    store_stats(to_z2, ROWS, stats)


def join_near(near, from_x, from_z, stats):
    return call(
        join_near_kernel,
        out_shape=[
            jax.ShapeDtypeStruct((SENT, KV), jnp.bfloat16),
            jax.ShapeDtypeStruct((ROWS, KV), jnp.float32),
            jax.ShapeDtypeStruct((LANES, LANES), jnp.float32),
        ],
        name="join_near",
    )(near, from_x, from_z, stats)


def finish_kernel(stats_ref, own_ref, other_ref, up_ref, *rest):
    out_ref, rows_ref, lifted_ref = rest[-3:]
    weights, _ = weigh(stats_ref[group(0)], load_stats(other_ref, ROWS)[group(2)])
    for part, rows in joined(((own_ref, 0), (other_ref, 0)), weights):
        for tile in range(4):
            rows_ref[tile, part, :] = rows[:, tile * LANES : (tile + 1) * LANES]
    for head in range(HEADS):
        attended = jnp.concatenate(
            [rows_ref[tile, pl.ds(head, PAIRS, stride=HEADS), :] for tile in range(4)], axis=1
        ).astype(jnp.bfloat16)
        lifted_ref[pl.ds(head, PAIRS, stride=HEADS), :] = jnp.dot(
            attended, up_ref[head], preferred_element_type=jnp.float32
        )
    for step in range(4):
        for local in range(2):
            row = (local * 4 + step) * HEADS
            out_ref[step, local] = lifted_ref[row : row + HEADS, :].astype(jnp.bfloat16)


def finish(chunk, stats, own, other, up, before):
    specs = [whole((LANES, LANES)), whole((ROWS, KV)), whole((SENT, KV))]
    specs.append(whole((HEADS, KV, 128)))
    args = [stats, own, other, up]
    aliases = {}
    if before is not None:
        specs.append(pl.BlockSpec(memory_space=pl.ANY))
        args.append(before)
        aliases = {len(args) - 1: 0}
    return call(
        finish_kernel,
        grid=(1,),
        in_specs=specs,
        out_specs=pl.BlockSpec((4, 2, HEADS, 128), lambda _: (0, chunk, 0, 0)),
        out_shape=jax.ShapeDtypeStruct((4, 4, HEADS, 128), jnp.bfloat16),
        scratch_shapes=[
            pltpu.VMEM((4, ROWS, LANES), jnp.float32),
            pltpu.VMEM((ROWS, 128), jnp.float32),
        ],
        input_output_aliases=aliases,
        name="finish",
        us=1.2,
    )(*args)


def pair_cores_kernel(own_ref, core_ref, out_ref):
    own = lax.axis_index("req") % 2
    out_ref[own] = own_ref[...]
    out_ref[1 - own] = core_ref[...]


def pair_cores(own, core):
    return call(
        pair_cores_kernel,
        out_shape=jax.ShapeDtypeStruct((2, *own.shape), own.dtype),
        name="pair_cores",
    )(own, core)


def assemble_kernel(_, here_ref, there_ref, out_ref):
    row = lax.axis_index("req") // 2
    for core in range(2):
        for place, ref in ((row, here_ref), (1 - row, there_ref)):
            start = pl.multiple_of((2 * place + core) * 128, 128)
            out_ref[:, pl.ds(start, 128), :] = ref[core]


def assemble(earlier, here, there):
    return call(
        assemble_kernel,
        in_specs=[pl.BlockSpec(memory_space=pl.ANY)] + [pl.BlockSpec()] * 2,
        out_shape=jax.ShapeDtypeStruct((HEADS, KV, 128), jnp.bfloat16),
        name="assemble_up",
        us=1.0,
    )(earlier, here, there)


def index_kernel(offsets, table_ref, *refs):
    arrays = refs[:16]
    key_ref, out_ref = refs[16:]
    request = pl.program_id(0)
    local = request % 2
    lane = lax.broadcasted_iota(jnp.int32, (64, LANES), 1)

    def work(members):
        columns = []
        for r, at in members:
            rows = r[at + ROWS : at + SENT, :LANES].astype(jnp.float32)
            rows = jnp.concatenate([rows, jnp.zeros((LANES - PAIRS, LANES), jnp.float32)], axis=0)
            columns.append(rows.T[:8])
        columns = jnp.concatenate(columns, axis=0)
        query_rows, weight_rows = [], []
        for step in range(4):
            pair = local * 4 + step
            tail = jnp.concatenate(
                [r[pl.ds(at + pl.multiple_of(pair * HEADS, HEADS), HEADS), 512:] for r, at in members],
                axis=0,
            )
            tail = tail.astype(jnp.float32).reshape(8, 2, 8, LANES)
            first = tail[:, 0].reshape(64, LANES)
            second = tail[:, 1].reshape(64, LANES)
            query_rows.append(jnp.concatenate([first[:, 64:], second[:, 64:]], axis=1))
            weight_rows.append(
                jnp.sum(jnp.where(lane == pair, columns, 0.0), axis=1, keepdims=True)
            )
        queries = jnp.concatenate(query_rows, axis=0).astype(jnp.bfloat16)
        for part in range(4):
            at = slice(part * 512, (part + 1) * 512)
            products = lax.dot_general(
                queries,
                key_ref[0, at, :],
                (((1,), (1,)), ((), ())),
                preferred_element_type=jnp.float32,
            )
            position = part * 512 + lax.broadcasted_iota(jnp.int32, (1, 512), 1)
            for step in range(4):
                mine = jnp.maximum(products[step * 64 : (step + 1) * 64], 0.0)
                summed = jnp.sum(mine * weight_rows[step], axis=0, keepdims=True)
                out_ref[step, pl.ds(request, 1), at] = jnp.where(
                    position <= table_ref[step * 4 + request, 17], summed, 0.0
                )

    for chunk in range(CHUNKS):

        @pl.when(request // 2 == chunk)
        def _(members=list(zip(arrays[8 * chunk : 8 * chunk + 8], offsets[8 * chunk : 8 * chunk + 8]))):
            work(members)


def index_rows(table, gathered, index_keys):
    members = [*gathered[0], *gathered[1]]
    return call(
        functools.partial(index_kernel, tuple(at for _, at in members)),
        grid_spec=pltpu.PrefetchScalarGridSpec(
            num_scalar_prefetch=1,
            grid=(4,),
            in_specs=[whole(array.shape) for array, _ in members]
            + [pl.BlockSpec((1, 2048, 128), lambda i, _: (i, 0, 0))],
            out_specs=whole((4, 4, 2048)),
        ),
        out_shape=jax.ShapeDtypeStruct((4, 4, 2048), jnp.float32),
        name="index_scores",
        us=3.5,
    )(table, *(array for array, _ in members), index_keys)


def fast(
    latents,
    index_keys,
    queries,
    index_queries,
    index_weights,
    value_up_weight,
    selection,
    counts,
    lengths,
):
    def across_x(value):
        return lax.ppermute(value, "ctx", [(i, i ^ 1) for i in range(8)])

    def across_z(value, distance):
        return lax.ppermute(value, "ctx", [(i, i ^ (2 * distance)) for i in range(8)])

    def across_req(value, distance):
        return lax.ppermute(value, "req", [(i, i ^ distance) for i in range(4)])

    own0, own1, both = pack(queries, index_queries, index_weights)
    table = plan(after(selection, own0), counts, lengths)
    latents_t = jnp.transpose(latents, (0, 2, 1))

    x0 = across_x(both)
    z2c0, z1c0 = across_z(own0, 2), across_z(own0, 1)

    blocks_a = gather((0, 1), GATHER_LIMIT[0], table, latents_t)
    round1 = (x0, z2c0, z1c0, blocks_a)
    x12 = across_x(pair_up(after(z1c0, *round1), z2c0))
    z3c0 = across_z(after(z2c0, *round1), 1)
    z2c1 = across_z(after(own1, *round1), 2)
    blocks_b = gather((2, 3), GATHER_LIMIT[1], after(table, *round1), latents_t)

    up_core = across_req(after(value_up_weight, *round1), 1)

    round2 = (x12, z3c0, z2c1, blocks_b)
    x32 = across_x(pair_up(after(z3c0, *round2), z2c1))
    z1c1 = across_z(after(own1, *round2), 1)
    z3c1 = across_z(after(z2c1, *round2), 1)
    up_here = pair_cores(after(value_up_weight, *round2), up_core)
    up_there = across_req(up_here, 2)

    round3 = (x32, z1c1, z3c1)
    xz1c1 = across_x(after(z1c1, *round3))
    xz2c1 = second_of(after(x32, *round3))
    xz3c1 = across_z(xz2c1, 1)
    gathered = [
        [(own0, 0), (z1c0, 0), (z2c0, 0), (z3c0, 0), (x0, 0), (x12, 0), (x12, SENT), (x32, 0)],
        [(own1, 0), (z1c1, 0), (z2c1, 0), (z3c1, 0), (x0, SENT), (xz1c1, 0), (xz2c1, 0), (xz3c1, 0)],
    ]

    near0, far0, cross0, x5, z7, stats0 = attend(0, after(table, xz2c1), gathered[0], blocks_a, latents_t)
    x5, z7 = across_x(x5), across_z(z7, 1)
    near1, far1, cross1, x5c1, z7c1, stats1 = attend(1, after(table, stats0), gathered[1], blocks_b, latents_t)
    x5c1, z7c1 = across_x(x5c1), across_z(z7c1, 1)

    to_z, to_x, stats0 = join_cross(far0, cross0, after(x5, stats1), z7, stats0)
    from_x, from_z = across_x(to_x), across_z(to_z, 1)
    to_z, to_x, stats1 = join_cross(far1, cross1, after(x5c1, stats0), z7c1, stats1)
    from_xc1, from_zc1 = across_x(to_x), across_z(to_z, 1)
    index_scores = index_rows(after(table, stats1), gathered, index_keys)
    up = assemble(index_scores, up_here, up_there)
    message, mine0, stats0 = join_near(after(near0, index_scores), from_x, from_z, stats0)
    last0 = across_z(message, 2)
    message, mine1, stats1 = join_near(near1, from_xc1, from_zc1, stats1)
    last1 = across_z(message, 2)
    head_values = finish(0, stats0, mine0, last0, up, None)
    head_values = finish(1, stats1, mine1, last1, up, head_values)
    return (head_values, index_scores)


def compact_slots(owned_slot, local_block, capacity):
    ranking = jnp.cumsum(owned_slot.astype(jnp.int32), axis=-1) - 1
    places = jnp.arange(capacity, dtype=jnp.int32)
    chosen = (owned_slot[..., None, :] & (ranking[..., None, :] == places[:, None])).astype(
        jnp.int32
    )
    block_index = jnp.sum(chosen * local_block[..., None, :], axis=-1)
    filled = jnp.sum(chosen, axis=-1) > 0
    return (block_index, filled)


def per_device(
    latents,
    index_keys,
    queries,
    index_queries,
    index_weights,
    value_up_weight,
    selection,
    counts,
    lengths,
):
    own_shard = lax.axis_index("ctx")
    step_count, request_count, slot_count = selection.shape
    half_axis = lax.axis_size("ctx") // 2
    capacity = max(2, (slot_count - 2) // half_axis + 1)
    context_dev = latents.shape[1]
    row_width = latents.shape[2]
    blocks_dev = context_dev // BLOCK
    score_scale = QK_DIM ** (-0.5)
    all_query, all_index_query, all_index_weight = (
        lax.all_gather(queries, "ctx", axis=2, tiled=True),
        lax.all_gather(index_queries, "ctx", axis=2, tiled=True),
        lax.all_gather(index_weights, "ctx", axis=2, tiled=True),
    )
    step_ids = jnp.arange(step_count, dtype=jnp.int32)
    limits = lengths[None, :] + step_ids[:, None]
    token_pos = own_shard * context_dev + jnp.arange(context_dev, dtype=jnp.int32)
    products = jnp.einsum(
        "srhd,rcd->srhc", all_index_query, index_keys, preferred_element_type=jnp.float32
    )
    weighted = jnp.einsum(
        "srhc,srh->src", jnp.maximum(products, 0.0), all_index_weight.astype(jnp.float32)
    )
    index_scores = jnp.where(token_pos[None, None, :] <= limits[:, :, None], weighted, 0.0)
    local_block = selection - own_shard * blocks_dev
    slot_ids = jnp.arange(slot_count, dtype=jnp.int32)
    owned_slot = (
        (local_block >= 0)
        & (local_block < blocks_dev)
        & (slot_ids[None, None, :] < counts[:, :, None])
    )
    block_index, filled = compact_slots(owned_slot, local_block, capacity)
    block_tiles = latents.reshape(request_count, blocks_dev, BLOCK, row_width)
    request_numbers = jnp.arange(request_count, dtype=jnp.int32)[None, :, None]
    gathered = block_tiles[request_numbers, block_index].reshape(
        step_count, request_count, capacity * BLOCK, row_width
    )
    positions = (block_index + own_shard * blocks_dev)[..., None] * BLOCK + jnp.arange(
        BLOCK, dtype=jnp.int32
    )
    usable = filled[..., None] & (positions <= limits[:, :, None, None])
    usable = usable.reshape(step_count, request_count, 1, capacity * BLOCK)
    scores = (
        jnp.einsum("srhl,srtl->srht", all_query, gathered, preferred_element_type=jnp.float32)
        * score_scale
    )
    scores = jnp.where(usable, scores, -1e30)
    peak_score = jnp.max(scores, axis=-1)
    exp_weights = jnp.where(usable, jnp.exp(scores - peak_score[..., None]), 0.0)
    row_total = jnp.sum(exp_weights, axis=-1)
    mixed_rows = jnp.einsum(
        "srht,srtk->srhk",
        exp_weights.astype(jnp.bfloat16),
        gathered[..., :KV],
        preferred_element_type=jnp.float32,
    )
    global_peak = lax.pmax(peak_score, "ctx")
    shrink = jnp.exp(peak_score - global_peak)
    share_total, mixed_share = (
        lax.psum_scatter(
            (row_total * shrink).astype(jnp.bfloat16), "ctx", scatter_dimension=2, tiled=True
        ).astype(jnp.float32),
        lax.psum_scatter(
            (mixed_rows * shrink[..., None]).astype(jnp.bfloat16),
            "ctx",
            scatter_dimension=2,
            tiled=True,
        ).astype(jnp.float32),
    )
    attended_output = (mixed_share / share_total[..., None]).astype(jnp.bfloat16)
    complete_up_matrix = lax.all_gather(value_up_weight, "req", axis=1, tiled=True)
    lifted_values = jnp.einsum(
        "xefy,fym->xefm", attended_output, complete_up_matrix, preferred_element_type=jnp.float32
    )
    head_values = lifted_values.astype(jnp.bfloat16)
    return (head_values, index_scores)


def solution(mesh):
    placed = (
        P("req", "ctx", None),
        P("req", "ctx", None),
        P(None, "req", "ctx", None),
        P(None, "req", "ctx", None),
        P(None, "req", "ctx"),
        P("ctx", "req", None),
        P(None, "req", None),
        P(None, "req"),
        P("req"),
    )
    sizes = dict(mesh.shape)
    plan_here = fast if (sizes["ctx"], sizes["req"]) == (8, 4) else per_device
    return jax.shard_map(
        plan_here,
        mesh=mesh,
        in_specs=placed,
        out_specs=(P(None, "req", "ctx", None), P(None, "req", "ctx")),
        check_vma=False,
    )
```

```python
import functools

import jax
import jax.numpy as jnp
from jax import lax
from jax.experimental import pallas as pl
from jax.experimental.pallas import tpu as pltpu
from jax.sharding import PartitionSpec as P

KV = 512
QK_DIM = 192
BLOCK = 64
VMEM_LIMIT = 16 * 1024 * 1024
PACK_LIMIT = 63_000_000
ATTEND_LIMIT = 24_000_000
TABLE = 32
GATHER_LIMIT = (46_000_000, 38_000_000)
SHORT = 4

CHUNKS = 2
PAIRS = 8
HEADS = 16
ROWS = PAIRS * HEADS
EXTRA = 8
SENT = ROWS + EXTRA
WIDE = 640
SLOTS = 8
LANES = 128


def call(body, limit=VMEM_LIMIT, us=0.3, **kwargs):
    return pl.pallas_call(
        body,
        cost_estimate=pl.CostEstimate(
            flops=int(us * 1e9), bytes_accessed=int(us * 3e6), transcendentals=0
        ),
        compiler_params=pltpu.CompilerParams(vmem_limit_bytes=limit),
        **kwargs,
    )


def after(value, *earlier):
    return lax.optimization_barrier((value, *earlier))[0]


def whole(shape):
    return pl.BlockSpec(shape, lambda *_: (0,) * len(shape))


def pack_kernel(q_hbm, iq_hbm, iw_hbm, out0_ref, out1_ref, both_ref, q_ref, iq_ref, iw_ref, sems):
    small = pltpu.make_async_copy(iw_hbm, iw_ref, sems.at[4])
    small.start()
    copies = []
    for chunk in range(CHUNKS):
        requests = pl.ds(2 * chunk, 2)
        copies.append(
            (
                pltpu.make_async_copy(
                    q_hbm.at[:, requests], q_ref.at[chunk], sems.at[2 * chunk]
                ),
                pltpu.make_async_copy(
                    iq_hbm.at[:, requests], iq_ref.at[chunk], sems.at[2 * chunk + 1]
                ),
            )
        )
        for copy in copies[-1]:
            copy.start()
    small.wait()
    for chunk, out_ref in enumerate((out0_ref, out1_ref)):
        for copy in copies[chunk]:
            copy.wait()
        rows = []
        for local in range(2):
            for step in range(4):
                row = (local * 4 + step) * HEADS
                query = q_ref[chunk, step, local]
                index_query = iq_ref[chunk, step, local]
                halves = jnp.concatenate([index_query[:, :64], index_query[:, 64:]], axis=0)
                out_ref[row : row + HEADS, :512] = query[:, :512]
                out_ref[row : row + HEADS, 512:] = jnp.concatenate(
                    [query[:, 512:], halves], axis=1
                )
                request = 2 * chunk + local
                rows.append(iw_ref[step, request : request + 1, :].astype(jnp.float32))
        weights = jnp.concatenate(rows, axis=0)
        weights = jnp.concatenate([weights, jnp.zeros((PAIRS, LANES - 8), jnp.float32)], axis=1)
        out_ref[ROWS:, :LANES] = weights.astype(jnp.bfloat16)
        out_ref[ROWS:, LANES:] = jnp.zeros((EXTRA, WIDE - LANES), jnp.bfloat16)
        both_ref[chunk * SENT : (chunk + 1) * SENT, :] = out_ref[...]


def pack(queries, index_queries, index_weights):
    bf16 = jnp.bfloat16
    return call(
        pack_kernel,
        limit=PACK_LIMIT,
        in_specs=[pl.BlockSpec(memory_space=pltpu.HBM)] * 3,
        out_shape=[jax.ShapeDtypeStruct((SENT, WIDE), bf16)] * 2
        + [jax.ShapeDtypeStruct((2 * SENT, WIDE), bf16)],
        scratch_shapes=[
            pltpu.VMEM((2, 4, 2, HEADS, 576), bf16),
            pltpu.VMEM((2, 4, 2, 8, 128), bf16),
            pltpu.VMEM((4, 4, 8), bf16),
            pltpu.SemaphoreType.DMA((5,)),
        ],
        name="pack",
        us=2,
    )(queries, index_queries, index_weights)


def pair_up_kernel(first_ref, second_ref, out_ref):
    out_ref[:SENT, :] = first_ref[...]
    out_ref[SENT:, :] = second_ref[...]


def pair_up(first, second):
    return call(
        pair_up_kernel,
        out_shape=jax.ShapeDtypeStruct((2 * SENT, WIDE), jnp.bfloat16),
        name="pair_up",
    )(first, second)


def second_of_kernel(both_ref, out_ref):
    out_ref[...] = both_ref[SENT:, :]


def second_of(both):
    return call(
        second_of_kernel,
        out_shape=jax.ShapeDtypeStruct((SENT, WIDE), jnp.bfloat16),
        name="second_of",
    )(both)


def plan_kernel(selection_ref, counts_ref, lengths_ref, out_ref):
    shard = lax.axis_index("ctx")
    row = lax.broadcasted_iota(jnp.int32, (16, 1), 0)
    count = jnp.zeros((16, 1), jnp.int32)
    limit = jnp.zeros((16, 1), jnp.int32)
    for step in range(4):
        for request in range(4):
            here = row == step * 4 + request
            count = jnp.where(here, counts_ref[step, request], count)
            limit = jnp.where(here, lengths_ref[request] + step - shard * 2048, limit)
    selection = jnp.concatenate([selection_ref[step] for step in range(4)], axis=0)
    local = selection - shard * (2048 // BLOCK)
    slot = lax.broadcasted_iota(jnp.int32, (16, 32), 1)
    owned = (local >= 0) & (local < 2048 // BLOCK) & (slot < count)
    before = (
        lax.broadcasted_iota(jnp.int32, (32, 32), 0) < lax.broadcasted_iota(jnp.int32, (32, 32), 1)
    ).astype(jnp.float32)
    lane = lax.broadcasted_iota(jnp.int32, (16, LANES), 1)
    table = jnp.full((16, LANES), -1, jnp.int32)
    most = jnp.zeros((16, 1), jnp.int32)
    for parity in range(2):
        mine = owned & (local % 2 == parity)
        mine_f = jnp.where(mine, 1.0, 0.0)
        rank = jnp.dot(mine_f, before, preferred_element_type=jnp.float32).astype(jnp.int32)
        for place in range(SLOTS):
            chosen = mine & (rank == place)
            found = jnp.sum(jnp.where(chosen, local // 2 + 1, 0), axis=1, keepdims=True) - 1
            table = jnp.where(lane == parity * SLOTS + place, found, table)
        most = jnp.maximum(most, jnp.sum(mine_f, axis=1, keepdims=True).astype(jnp.int32))
    table = jnp.where(lane == 16, most, table)
    table = jnp.where(lane == 17, limit, table)
    out_ref[...] = table[:, :TABLE]


def plan(selection, counts, lengths):
    smem = pl.BlockSpec(memory_space=pltpu.SMEM)
    return call(
        plan_kernel,
        in_specs=[pl.BlockSpec(), smem, smem],
        out_shape=jax.ShapeDtypeStruct((16, TABLE), jnp.int32),
        name="plan",
        us=0.9,
    )(selection, counts, lengths)


def split3(value):
    high = value.astype(jnp.bfloat16)
    rest = value - high.astype(jnp.float32)
    middle = rest.astype(jnp.bfloat16)
    low = (rest - middle.astype(jnp.float32)).astype(jnp.bfloat16)
    return high, middle, low


def store_stats(out_ref, row, stats):
    turned = stats.T[:PAIRS]
    for place, part in enumerate(split3(turned)):
        out_ref[row : row + PAIRS, place * LANES : (place + 1) * LANES] = part
    out_ref[row : row + PAIRS, 3 * LANES :] = jnp.zeros((PAIRS, LANES), jnp.bfloat16)


def load_stats(in_ref, row):
    parts = [
        in_ref[row : row + PAIRS, place * LANES : (place + 1) * LANES].astype(jnp.float32)
        for place in range(3)
    ]
    turned = (parts[0] + parts[1]) + parts[2]
    return jnp.concatenate([turned, jnp.zeros((LANES - PAIRS, LANES), jnp.float32)], axis=0).T


def gather_kernel(requests, table_ref, latent_hbm, out_ref, latent_ref, sems):
    copies = []
    for local, request in enumerate(requests):
        for part in range(4):
            rows = pl.ds(part * 144, 144)
            copies.append(
                pltpu.make_async_copy(
                    latent_hbm.at[request, rows],
                    latent_ref.at[local, rows],
                    sems.at[local * 4 + part],
                )
            )
    for copy in copies:
        copy.start()
    in_even = lax.broadcasted_iota(jnp.int32, (144, LANES), 1) < BLOCK
    for index, copy in enumerate(copies):
        copy.wait()
        local, part = divmod(index, 4)
        request = requests[local]
        rows = slice(part * 144, (part + 1) * 144)

        def tile(row, place, local=local, rows=rows):
            start = pl.multiple_of(jnp.maximum(table_ref[row, place], 0) * LANES, LANES)
            return latent_ref[local, rows, pl.ds(start, LANES)]

        def fill(places, local=local, request=request, rows=rows, tile=tile):
            for step in range(4):
                row = step * 4 + request
                for place in places:
                    out_ref[local * 4 + step, rows, place * LANES : (place + 1) * LANES] = jnp.where(
                        in_even, tile(row, place), tile(row, SLOTS + place)
                    )

        fill(range(SHORT))


def most_of(table_ref, request):
    most = table_ref[request, 16]
    for step in range(1, 4):
        most = jnp.maximum(most, table_ref[step * 4 + request, 16])
    return most


def gather(requests, limit, table, latents_t):
    bf16 = jnp.bfloat16
    count = len(requests)
    return call(
        functools.partial(gather_kernel, requests),
        limit=limit,
        in_specs=[pl.BlockSpec(memory_space=pltpu.SMEM), pl.BlockSpec(memory_space=pltpu.HBM)],
        out_shape=jax.ShapeDtypeStruct((4 * count, 576, SHORT * LANES), bf16),
        scratch_shapes=[
            pltpu.VMEM((count, 576, 2048), bf16),
            pltpu.SemaphoreType.DMA((4 * count,)),
        ],
        name="gather_blocks",
        us=2.6 * count,
    )(table, latents_t)


def attend_kernel(chunk, offsets, table_ref, *refs):
    q_refs = refs[:8]
    block_ref, latent_hbm = refs[8:10]
    near, far, cross, send_x, send_z, stats_ref = refs[10:16]
    score_ref, weight_ref, latent_ref, wide_ref, sem = refs[16:]
    lane = lax.broadcasted_iota(jnp.int32, (LANES, LANES), 1)
    position = lax.broadcasted_iota(jnp.int32, (1, LANES), 1)
    stats_ref[...] = jnp.zeros((LANES, LANES), jnp.float32)

    def query_of(pair):
        return jnp.concatenate(
            [r[at + pair * HEADS : at + (pair + 1) * HEADS, :576] for r, at in zip(q_refs, offsets)],
            axis=0,
        )

    def scores_of(pair, row, blocks, tiles):
        bias = []
        for place in range(tiles):
            at = jnp.where(position < BLOCK, table_ref[row, place], table_ref[row, SLOTS + place])
            usable = (at >= 0) & (at * LANES + position <= table_ref[row, 17])
            bias.append(jnp.where(usable, 0.0, -1e30))
        scores = jnp.dot(query_of(pair), blocks, preferred_element_type=jnp.float32)
        return scores * (QK_DIM**-0.5) + jnp.concatenate(bias, axis=1)

    def weights_of(pair, scores):
        peak = jnp.maximum(jnp.max(scores, axis=1, keepdims=True), -1e29)
        weights = jnp.exp(scores - peak)
        total = jnp.maximum(jnp.sum(weights, axis=1, keepdims=True), 1e-30)
        stats_ref[...] = jnp.where(lane == pair, peak + jnp.log(total), stats_ref[...])
        return weights.astype(jnp.bfloat16), 1.0 / total

    def mix(pair, weights, blocks, scale):
        mixed = lax.dot_general(
            weights, blocks, (((1,), (1,)), ((), ())), preferred_element_type=jnp.float32
        )
        mixed = (mixed * scale).astype(jnp.bfloat16)
        row = pair * HEADS
        for out, places in (
            (near, (0, 2)),
            (far, (1, 3)),
            (cross, (4, 6)),
            (send_x, (5,)),
            (send_z, (7,)),
        ):
            for half, place in enumerate(places):
                at = half * ROWS + row
                out[at : at + HEADS, :] = mixed[place * HEADS : (place + 1) * HEADS]

    def short(local, request):
        for step in range(4):
            pair = local * 4 + step
            score_ref[step] = scores_of(pair, step * 4 + request, block_ref[pair], SHORT)
        scales = []
        for step in range(4):
            weight_ref[step], scale = weights_of(local * 4 + step, score_ref[step])
            scales.append(scale)
        for step in range(4):
            pair = local * 4 + step
            mix(pair, weight_ref[step], block_ref[pair, :KV], scales[step])

    def long(local, request):
        copy = pltpu.make_async_copy(latent_hbm.at[request], latent_ref, sem.at[0])
        copy.start()
        copy.wait()
        in_even = lax.broadcasted_iota(jnp.int32, (576, LANES), 1) < BLOCK
        for step in range(4):
            pair, row = local * 4 + step, step * 4 + request

            def tile(place, row=row):
                start = pl.multiple_of(jnp.maximum(table_ref[row, place], 0) * LANES, LANES)
                return latent_ref[:, pl.ds(start, LANES)]

            for place in range(SLOTS):
                wide_ref[:, place * LANES : (place + 1) * LANES] = jnp.where(
                    in_even, tile(place), tile(SLOTS + place)
                )
            weights, scale = weights_of(pair, scores_of(pair, row, wide_ref[...], SLOTS))
            mix(pair, weights, wide_ref[:KV], scale)

    for local in range(2):
        request = 2 * chunk + local
        most = most_of(table_ref, request)

        @pl.when(most <= SHORT)
        def _(local=local, request=request):
            short(local, request)

        @pl.when(most > SHORT)
        def _(local=local, request=request):
            long(local, request)

    store_stats(send_x, ROWS, stats_ref[...])
    store_stats(send_z, ROWS, stats_ref[...])


def attend(chunk, table, gathered_queries, blocks, latents_t):
    bf16 = jnp.bfloat16
    return call(
        functools.partial(attend_kernel, chunk, tuple(at for _, at in gathered_queries)),
        limit=ATTEND_LIMIT,
        in_specs=[pl.BlockSpec(memory_space=pltpu.SMEM)] + [pl.BlockSpec()] * 9
        + [pl.BlockSpec(memory_space=pltpu.HBM)],
        out_shape=[
            jax.ShapeDtypeStruct((2 * ROWS, KV), bf16),
            jax.ShapeDtypeStruct((2 * ROWS, KV), bf16),
            jax.ShapeDtypeStruct((2 * ROWS, KV), bf16),
            jax.ShapeDtypeStruct((SENT, KV), bf16),
            jax.ShapeDtypeStruct((SENT, KV), bf16),
            jax.ShapeDtypeStruct((LANES, LANES), jnp.float32),
        ],
        scratch_shapes=[
            pltpu.VMEM((4, LANES, SHORT * LANES), jnp.float32),
            pltpu.VMEM((4, LANES, SHORT * LANES), bf16),
            pltpu.VMEM((576, 2048), bf16),
            pltpu.VMEM((576, SLOTS * LANES), bf16),
            pltpu.SemaphoreType.DMA((1,)),
        ],
        name="attend",
        us=3.6,
    )(table, *(array for array, _ in gathered_queries), blocks, latents_t)


def group(number):
    return slice(number * HEADS, (number + 1) * HEADS)


def weigh(*stats):
    peak = functools.reduce(jnp.maximum, stats)
    weights = [jnp.exp(value - peak) for value in stats]
    total = functools.reduce(jnp.add, weights)
    return [value / total for value in weights], peak + jnp.log(total)


def joined(parts, weights):
    for pair in range(PAIRS):
        rows = None
        for (ref, start), weight in zip(parts, weights):
            at = start + pair * HEADS
            part = ref[at : at + HEADS, :].astype(jnp.float32) * weight[:, pair : pair + 1]
            rows = part if rows is None else rows + part
        yield slice(pair * HEADS, (pair + 1) * HEADS), rows


def stack(stats, new):
    return jnp.concatenate([new.get(number, stats[group(number)]) for number in range(8)], axis=0)


def join_cross_kernel(far, cross, from_x, from_z, stats_ref, to_z, to_x, out_stats):
    stats = stats_ref[...]
    weights, lse1 = weigh(stats[group(1)], load_stats(from_x, ROWS)[group(5)])
    for rows, value in joined(((far, 0), (from_x, 0)), weights):
        to_z[rows, :] = value.astype(jnp.bfloat16)
    to_z[ROWS : 2 * ROWS, :] = far[ROWS:, :]
    weights, lse6 = weigh(stats[group(6)], load_stats(from_z, ROWS)[group(7)])
    to_x[:ROWS, :] = cross[:ROWS, :]
    for rows, value in joined(((cross, ROWS), (from_z, 0)), weights):
        to_x[ROWS + rows.start : ROWS + rows.stop, :] = value.astype(jnp.bfloat16)
    stats = stack(stats, {1: lse1, 6: lse6})
    out_stats[...] = stats
    store_stats(to_z, 2 * ROWS, stats)
    store_stats(to_x, 2 * ROWS, stats)


def join_cross(far, cross, from_x, from_z, stats):
    message = jax.ShapeDtypeStruct((2 * ROWS + EXTRA, KV), jnp.bfloat16)
    return call(
        join_cross_kernel,
        out_shape=[message, message, jax.ShapeDtypeStruct((LANES, LANES), jnp.float32)],
        name="join_cross",
    )(far, cross, from_x, from_z, stats)


def join_near_kernel(near, from_x, from_z, stats_ref, to_z2, mine, out_stats):
    stats, stats_x, stats_z = (
        stats_ref[...],
        load_stats(from_x, 2 * ROWS),
        load_stats(from_z, 2 * ROWS),
    )
    weights, lse2 = weigh(stats[group(2)], stats_x[group(6)], stats_z[group(3)])
    for rows, value in joined(((near, ROWS), (from_x, ROWS), (from_z, ROWS)), weights):
        to_z2[rows, :] = value.astype(jnp.bfloat16)
    weights, lse0 = weigh(stats[group(0)], stats_x[group(4)], stats_z[group(1)])
    for rows, value in joined(((near, 0), (from_x, 0), (from_z, 0)), weights):
        mine[rows, :] = value
    stats = stack(stats, {0: lse0, 2: lse2})
    out_stats[...] = stats
    store_stats(to_z2, ROWS, stats)


def join_near(near, from_x, from_z, stats):
    return call(
        join_near_kernel,
        out_shape=[
            jax.ShapeDtypeStruct((SENT, KV), jnp.bfloat16),
            jax.ShapeDtypeStruct((ROWS, KV), jnp.float32),
            jax.ShapeDtypeStruct((LANES, LANES), jnp.float32),
        ],
        name="join_near",
    )(near, from_x, from_z, stats)


def finish_kernel(stats_ref, own_ref, other_ref, up_ref, *rest):
    out_ref, rows_ref, lifted_ref = rest[-3:]
    weights, _ = weigh(stats_ref[group(0)], load_stats(other_ref, ROWS)[group(2)])
    for part, rows in joined(((own_ref, 0), (other_ref, 0)), weights):
        for tile in range(4):
            rows_ref[tile, part, :] = rows[:, tile * LANES : (tile + 1) * LANES]
    for head in range(HEADS):
        attended = jnp.concatenate(
            [rows_ref[tile, pl.ds(head, PAIRS, stride=HEADS), :] for tile in range(4)], axis=1
        ).astype(jnp.bfloat16)
        lifted_ref[pl.ds(head, PAIRS, stride=HEADS), :] = jnp.dot(
            attended, up_ref[head], preferred_element_type=jnp.float32
        )
    for step in range(4):
        for local in range(2):
            row = (local * 4 + step) * HEADS
            out_ref[step, local] = lifted_ref[row : row + HEADS, :].astype(jnp.bfloat16)


def finish(chunk, stats, own, other, up, before):
    specs = [whole((LANES, LANES)), whole((ROWS, KV)), whole((SENT, KV))]
    specs.append(whole((HEADS, KV, 128)))
    args = [stats, own, other, up]
    aliases = {}
    if before is not None:
        specs.append(pl.BlockSpec(memory_space=pl.ANY))
        args.append(before)
        aliases = {len(args) - 1: 0}
    return call(
        finish_kernel,
        grid=(1,),
        in_specs=specs,
        out_specs=pl.BlockSpec((4, 2, HEADS, 128), lambda _: (0, chunk, 0, 0)),
        out_shape=jax.ShapeDtypeStruct((4, 4, HEADS, 128), jnp.bfloat16),
        scratch_shapes=[
            pltpu.VMEM((4, ROWS, LANES), jnp.float32),
            pltpu.VMEM((ROWS, 128), jnp.float32),
        ],
        input_output_aliases=aliases,
        name="finish",
        us=1.2,
    )(*args)


def pair_cores_kernel(own_ref, core_ref, out_ref):
    own = lax.axis_index("req") % 2
    out_ref[own] = own_ref[...]
    out_ref[1 - own] = core_ref[...]


def pair_cores(own, core):
    return call(
        pair_cores_kernel,
        out_shape=jax.ShapeDtypeStruct((2, *own.shape), own.dtype),
        name="pair_cores",
    )(own, core)


def assemble_kernel(_, here_ref, there_ref, out_ref):
    row = lax.axis_index("req") // 2
    for core in range(2):
        for place, ref in ((row, here_ref), (1 - row, there_ref)):
            start = pl.multiple_of((2 * place + core) * 128, 128)
            out_ref[:, pl.ds(start, 128), :] = ref[core]


def assemble(earlier, here, there):
    return call(
        assemble_kernel,
        in_specs=[pl.BlockSpec(memory_space=pl.ANY)] + [pl.BlockSpec()] * 2,
        out_shape=jax.ShapeDtypeStruct((HEADS, KV, 128), jnp.bfloat16),
        name="assemble_up",
        us=1.0,
    )(earlier, here, there)


def index_kernel(offsets, table_ref, *refs):
    arrays = refs[:16]
    key_ref, out_ref = refs[16:]
    request = pl.program_id(0)
    local = request % 2
    lane = lax.broadcasted_iota(jnp.int32, (64, LANES), 1)

    def work(members):
        columns = []
        for r, at in members:
            rows = r[at + ROWS : at + SENT, :LANES].astype(jnp.float32)
            rows = jnp.concatenate([rows, jnp.zeros((LANES - PAIRS, LANES), jnp.float32)], axis=0)
            columns.append(rows.T[:8])
        columns = jnp.concatenate(columns, axis=0)
        query_rows, weight_rows = [], []
        for step in range(4):
            pair = local * 4 + step
            tail = jnp.concatenate(
                [r[pl.ds(at + pl.multiple_of(pair * HEADS, HEADS), HEADS), 512:] for r, at in members],
                axis=0,
            )
            tail = tail.astype(jnp.float32).reshape(8, 2, 8, LANES)
            first = tail[:, 0].reshape(64, LANES)
            second = tail[:, 1].reshape(64, LANES)
            query_rows.append(jnp.concatenate([first[:, 64:], second[:, 64:]], axis=1))
            weight_rows.append(
                jnp.sum(jnp.where(lane == pair, columns, 0.0), axis=1, keepdims=True)
            )
        queries = jnp.concatenate(query_rows, axis=0).astype(jnp.bfloat16)
        for part in range(4):
            at = slice(part * 512, (part + 1) * 512)
            products = lax.dot_general(
                queries,
                key_ref[0, at, :],
                (((1,), (1,)), ((), ())),
                preferred_element_type=jnp.float32,
            )
            position = part * 512 + lax.broadcasted_iota(jnp.int32, (1, 512), 1)
            for step in range(4):
                mine = jnp.maximum(products[step * 64 : (step + 1) * 64], 0.0)
                summed = jnp.sum(mine * weight_rows[step], axis=0, keepdims=True)
                out_ref[step, pl.ds(request, 1), at] = jnp.where(
                    position <= table_ref[step * 4 + request, 17], summed, 0.0
                )

    for chunk in range(CHUNKS):

        @pl.when(request // 2 == chunk)
        def _(members=list(zip(arrays[8 * chunk : 8 * chunk + 8], offsets[8 * chunk : 8 * chunk + 8]))):
            work(members)


def index_rows(table, gathered, index_keys):
    members = [*gathered[0], *gathered[1]]
    return call(
        functools.partial(index_kernel, tuple(at for _, at in members)),
        grid_spec=pltpu.PrefetchScalarGridSpec(
            num_scalar_prefetch=1,
            grid=(4,),
            in_specs=[whole(array.shape) for array, _ in members]
            + [pl.BlockSpec((1, 2048, 128), lambda i, _: (i, 0, 0))],
            out_specs=whole((4, 4, 2048)),
        ),
        out_shape=jax.ShapeDtypeStruct((4, 4, 2048), jnp.float32),
        name="index_scores",
        us=3.5,
    )(table, *(array for array, _ in members), index_keys)


def fast(
    latents,
    index_keys,
    queries,
    index_queries,
    index_weights,
    value_up_weight,
    selection,
    counts,
    lengths,
):
    def across_x(value):
        return lax.ppermute(value, "ctx", [(i, i ^ 1) for i in range(8)])

    def across_z(value, distance):
        return lax.ppermute(value, "ctx", [(i, i ^ (2 * distance)) for i in range(8)])

    def across_req(value, distance):
        return lax.ppermute(value, "req", [(i, i ^ distance) for i in range(4)])

    own0, own1, both = pack(queries, index_queries, index_weights)
    table = plan(after(selection, own0), counts, lengths)
    latents_t = jnp.transpose(latents, (0, 2, 1))

    x0 = across_x(both)
    z2c0, z1c0 = across_z(own0, 2), across_z(own0, 1)

    blocks_a = gather((0, 1), GATHER_LIMIT[0], table, latents_t)
    round1 = (x0, z2c0, z1c0, blocks_a)
    x12 = across_x(pair_up(after(z1c0, *round1), z2c0))
    z3c0 = across_z(after(z2c0, *round1), 1)
    z2c1 = across_z(after(own1, *round1), 2)
    blocks_b = gather((2, 3), GATHER_LIMIT[1], after(table, *round1), latents_t)

    up_core = across_req(after(value_up_weight, *round1), 1)

    round2 = (x12, z3c0, z2c1, blocks_b)
    xz3c0 = across_x(after(z3c0, *round2))
    xz2c1 = across_x(after(z2c1, *round2))
    z1c1 = across_z(after(own1, *round2), 1)
    z3c1 = across_z(after(z2c1, *round2), 1)
    up_here = pair_cores(after(value_up_weight, *round2), up_core)
    up_there = across_req(up_here, 2)

    xz1c1 = across_x(z1c1)
    xz3c1 = across_z(xz2c1, 1)
    gathered = [
        [(own0, 0), (z1c0, 0), (z2c0, 0), (z3c0, 0), (x0, 0), (x12, 0), (x12, SENT), (xz3c0, 0)],
        [(own1, 0), (z1c1, 0), (z2c1, 0), (z3c1, 0), (x0, SENT), (xz1c1, 0), (xz2c1, 0), (xz3c1, 0)],
    ]

    near0, far0, cross0, x5, z7, stats0 = attend(
        0, after(table, z1c1), gathered[0], blocks_a, latents_t
    )
    x5, z7 = across_x(x5), across_z(z7, 1)
    near1, far1, cross1, x5c1, z7c1, stats1 = attend(1, after(table, stats0), gathered[1], blocks_b, latents_t)
    x5c1, z7c1 = across_x(x5c1), across_z(z7c1, 1)

    to_z, to_x, stats0 = join_cross(far0, cross0, after(x5, stats1), z7, stats0)
    from_x, from_z = across_x(to_x), across_z(to_z, 1)
    to_z, to_x, stats1 = join_cross(far1, cross1, after(x5c1, stats0), z7c1, stats1)
    from_xc1, from_zc1 = across_x(to_x), across_z(to_z, 1)
    index_scores = index_rows(after(table, stats1), gathered, index_keys)
    up = assemble(index_scores, up_here, up_there)
    message, mine0, stats0 = join_near(after(near0, index_scores), from_x, from_z, stats0)
    last0 = across_z(message, 2)
    message, mine1, stats1 = join_near(near1, from_xc1, from_zc1, stats1)
    last1 = across_z(message, 2)
    head_values = finish(0, stats0, mine0, last0, up, None)
    head_values = finish(1, stats1, mine1, last1, up, head_values)
    return (head_values, index_scores)


def compact_slots(owned_slot, local_block, capacity):
    ranking = jnp.cumsum(owned_slot.astype(jnp.int32), axis=-1) - 1
    places = jnp.arange(capacity, dtype=jnp.int32)
    chosen = (owned_slot[..., None, :] & (ranking[..., None, :] == places[:, None])).astype(
        jnp.int32
    )
    block_index = jnp.sum(chosen * local_block[..., None, :], axis=-1)
    filled = jnp.sum(chosen, axis=-1) > 0
    return (block_index, filled)


def per_device(
    latents,
    index_keys,
    queries,
    index_queries,
    index_weights,
    value_up_weight,
    selection,
    counts,
    lengths,
):
    own_shard = lax.axis_index("ctx")
    step_count, request_count, slot_count = selection.shape
    half_axis = lax.axis_size("ctx") // 2
    capacity = max(2, (slot_count - 2) // half_axis + 1)
    context_dev = latents.shape[1]
    row_width = latents.shape[2]
    blocks_dev = context_dev // BLOCK
    score_scale = QK_DIM ** (-0.5)
    all_query, all_index_query, all_index_weight = (
        lax.all_gather(queries, "ctx", axis=2, tiled=True),
        lax.all_gather(index_queries, "ctx", axis=2, tiled=True),
        lax.all_gather(index_weights, "ctx", axis=2, tiled=True),
    )
    step_ids = jnp.arange(step_count, dtype=jnp.int32)
    limits = lengths[None, :] + step_ids[:, None]
    token_pos = own_shard * context_dev + jnp.arange(context_dev, dtype=jnp.int32)
    products = jnp.einsum(
        "srhd,rcd->srhc", all_index_query, index_keys, preferred_element_type=jnp.float32
    )
    weighted = jnp.einsum(
        "srhc,srh->src", jnp.maximum(products, 0.0), all_index_weight.astype(jnp.float32)
    )
    index_scores = jnp.where(token_pos[None, None, :] <= limits[:, :, None], weighted, 0.0)
    local_block = selection - own_shard * blocks_dev
    slot_ids = jnp.arange(slot_count, dtype=jnp.int32)
    owned_slot = (
        (local_block >= 0)
        & (local_block < blocks_dev)
        & (slot_ids[None, None, :] < counts[:, :, None])
    )
    block_index, filled = compact_slots(owned_slot, local_block, capacity)
    block_tiles = latents.reshape(request_count, blocks_dev, BLOCK, row_width)
    request_numbers = jnp.arange(request_count, dtype=jnp.int32)[None, :, None]
    gathered = block_tiles[request_numbers, block_index].reshape(
        step_count, request_count, capacity * BLOCK, row_width
    )
    positions = (block_index + own_shard * blocks_dev)[..., None] * BLOCK + jnp.arange(
        BLOCK, dtype=jnp.int32
    )
    usable = filled[..., None] & (positions <= limits[:, :, None, None])
    usable = usable.reshape(step_count, request_count, 1, capacity * BLOCK)
    scores = (
        jnp.einsum("srhl,srtl->srht", all_query, gathered, preferred_element_type=jnp.float32)
        * score_scale
    )
    scores = jnp.where(usable, scores, -1e30)
    peak_score = jnp.max(scores, axis=-1)
    exp_weights = jnp.where(usable, jnp.exp(scores - peak_score[..., None]), 0.0)
    row_total = jnp.sum(exp_weights, axis=-1)
    mixed_rows = jnp.einsum(
        "srht,srtk->srhk",
        exp_weights.astype(jnp.bfloat16),
        gathered[..., :KV],
        preferred_element_type=jnp.float32,
    )
    global_peak = lax.pmax(peak_score, "ctx")
    shrink = jnp.exp(peak_score - global_peak)
    share_total, mixed_share = (
        lax.psum_scatter(
            (row_total * shrink).astype(jnp.bfloat16), "ctx", scatter_dimension=2, tiled=True
        ).astype(jnp.float32),
        lax.psum_scatter(
            (mixed_rows * shrink[..., None]).astype(jnp.bfloat16),
            "ctx",
            scatter_dimension=2,
            tiled=True,
        ).astype(jnp.float32),
    )
    attended_output = (mixed_share / share_total[..., None]).astype(jnp.bfloat16)
    complete_up_matrix = lax.all_gather(value_up_weight, "req", axis=1, tiled=True)
    lifted_values = jnp.einsum(
        "xefy,fym->xefm", attended_output, complete_up_matrix, preferred_element_type=jnp.float32
    )
    head_values = lifted_values.astype(jnp.bfloat16)
    return (head_values, index_scores)


def solution(mesh):
    placed = (
        P("req", "ctx", None),
        P("req", "ctx", None),
        P(None, "req", "ctx", None),
        P(None, "req", "ctx", None),
        P(None, "req", "ctx"),
        P("ctx", "req", None),
        P(None, "req", None),
        P(None, "req"),
        P("req"),
    )
    sizes = dict(mesh.shape)
    plan_here = fast if (sizes["ctx"], sizes["req"]) == (8, 4) else per_device
    return jax.shard_map(
        plan_here,
        mesh=mesh,
        in_specs=placed,
        out_specs=(P(None, "req", "ctx", None), P(None, "req", "ctx")),
        check_vma=False,
    )
```
